128 devices in a mesh: ctx: 16 (over y, x_hi, core), tp: 8 (over z, x_lo).
Axes of the slice: x: 4 (x_hi: 2, x_lo: 2; x = x_hi * 2 + x_lo), y: 4, z: 4, core: 2. Of those that a mesh axis runs over, the one named last changes fastest.
Arguments:
- query_gate: bfloat16 [4096, 16384], P('tp', 'ctx'), may hold values from -6 to 6
- key_gate: bfloat16 [4096, 16384], P('tp', 'ctx'), may hold values from -6 to 6
- value_in: bfloat16 [4096, 16384], P('tp', 'ctx'), may hold values from -6 to 6
- grad_out: bfloat16 [4096, 16384], P('tp', 'ctx'), may hold values from -6 to 6
- skip_bias: float32 [4096], P('tp'), may hold values from -1 to 1
- decay: float32 [256], P('tp'), may hold values from 6.1035156e-06 to 0.0333333333
- w_first: float32 [33, 64], replicated, may hold values from -1 to 1
- b_first: float32 [64], replicated, may hold values from -3.140625 to 3.140625
- w_second: float32 [64, 64], replicated, may hold values from -0.75 to 0.75
- b_second: float32 [64], replicated, may hold values from -3.140625 to 3.140625
- w_third: float32 [64, 256], replicated, may hold values from -0.75 to 0.75
Outputs:
- mixed_out: bfloat16 [4096, 16384], P('tp', 'ctx')
- grad_query: bfloat16 [4096, 16384], P('tp', 'ctx')
- grad_key: bfloat16 [4096, 16384], P('tp', 'ctx')
- grad_value: bfloat16 [4096, 16384], P('tp', 'ctx')
- grad_w_first: float32 [33, 64], replicated
- grad_b_first: float32 [64], replicated
- grad_w_second: float32 [64, 64], replicated
- grad_b_second: float32 [64], replicated
- grad_w_third: float32 [64, 256], replicated
The draws below stay inside these ranges and needn't reach their ends.
All inputs are finite; a program needn't handle non-finite values.
Results may differ from the reference program's by a relative error of at most 0.0064.
Values may be sent and summed in bfloat16 or wider, within the bound.
A program may use at most 128 MiB of HBM per device.

```python
import math
import jax
import jax.numpy as jnp
from jax import lax

CH = 4096
GSIZE = 16
GROUPS = 256
ORDER = 64
BANDS = 16
EMB = 33
LEN = 16384


def draw_decay(key, part):
    key = jax.random.fold_in(key, 7)
    pick_key, slow_key, fast_key = jax.random.split(key, 3)
    keep_share = 0.5
    is_slow = jax.random.uniform(pick_key, (GROUPS,), dtype=jnp.float32) < keep_share
    slow_rate = jax.random.uniform(slow_key, (GROUPS,), dtype=jnp.float32, minval=0.1, maxval=1.5) / LEN
    fast_rate = jax.random.uniform(fast_key, (GROUPS,), dtype=jnp.float32, minval=1.0 / 50.0, maxval=1.0 / 30.0)
    return jnp.where(is_slow, slow_rate, fast_rate).astype(jnp.float32)


def shard_levels(rng, extent, cuts, low, high):
    loudness = 1.0
    for position, shards_of in cuts:
        heights = jax.random.uniform(jax.random.fold_in(jax.random.fold_in(rng, 6), position), (shards_of,), jnp.float32, low / len(cuts), high / len(cuts))
        loudness = loudness * jnp.repeat(jnp.exp(heights), extent[position] // shards_of).reshape((-1,) + (1,) * (len(extent) - 1 - position))
    return loudness


def scatter_about(key, dims, scale, bound, cuts=(), kind=jnp.bfloat16):
    values = scale * jax.random.normal(key, dims, jnp.float32)
    if cuts:
        values = values * shard_levels(key, dims, cuts, -0.22, 0.18)
    return jnp.clip(values, -bound, bound).astype(kind)


def setup_inputs(seed: int = 0) -> dict:
    key_list = jax.random.split(jax.random.key(seed), 12)
    query_gate = scatter_about(key_list[0], (CH, LEN), 1.0, 6.0, ((0, 8), (1, 16)))
    key_gate = scatter_about(key_list[1], (CH, LEN), 1.0, 6.0, ((0, 8), (1, 16)))
    value_in = scatter_about(key_list[2], (CH, LEN), 1.0, 6.0, ((0, 8), (1, 16)))
    grad_out = scatter_about(key_list[3], (CH, LEN), 1.0, 6.0, ((0, 8), (1, 16)))
    skip_bias = jnp.clip(jax.random.uniform(key_list[4], (CH,), jnp.float32, -1.0, 1.0) * shard_levels(key_list[4], (CH,), ((0, 8),), -0.4, 0.0), -1.0, 1.0)
    decay = draw_decay(jax.random.fold_in(key_list[11], 71), 0)
    w_first = scatter_about(key_list[6], (EMB, ORDER), EMB ** -0.5, 1.0, (), jnp.float32)
    b_first = jnp.clip(jax.random.uniform(key_list[7], (ORDER,), jnp.float32, -3.140625, 3.140625), -3.140625, 3.140625)
    w_second = scatter_about(key_list[8], (ORDER, ORDER), ORDER ** -0.5, 0.75, (), jnp.float32)
    b_second = jnp.clip(jax.random.uniform(key_list[9], (ORDER,), jnp.float32, -3.140625, 3.140625), -3.140625, 3.140625)
    w_third = scatter_about(key_list[10], (ORDER, GROUPS), ORDER ** -0.5, 0.75, (), jnp.float32)
    return dict(query_gate=query_gate, key_gate=key_gate, value_in=value_in, grad_out=grad_out, skip_bias=skip_bias, decay=decay, w_first=w_first, b_first=b_first, w_second=w_second, b_second=b_second, w_third=w_third)


HIGHEST_MODE = lax.Precision.HIGHEST

def wrapped_index(positions, multipliers, modulus):
    upper_part = multipliers // 256
    lower_part = multipliers % 256
    partial_term = positions * upper_part % modulus
    return (partial_term * 256 + positions * lower_part) % modulus

def position_features(start, count, seq_len, band_count):
    positions = start + lax.broadcasted_iota(jnp.int32, (count, 1), 0)
    multipliers = jnp.array([1 + 3 * seq_len // (8 * 2 ** band_idx) for band_idx in range(band_count)], dtype=jnp.int32)[None, :]
    phases = wrapped_index(positions, multipliers, seq_len).astype(jnp.float32) * (2.0 * math.pi / seq_len)
    ramp_col = positions.astype(jnp.float32) / seq_len
    return (jnp.concatenate([ramp_col, jnp.cos(phases), jnp.sin(phases)], axis=1), positions.astype(jnp.float32))

def filter_values(features, positions_f, seq_len, decay, w_one, b_one, w_two, b_two, w_three):
    hid_one = jnp.sin(jnp.dot(features, w_one, precision=HIGHEST_MODE, preferred_element_type=jnp.float32) + b_one)
    hid_two = jnp.sin(jnp.dot(hid_one, w_two, precision=HIGHEST_MODE, preferred_element_type=jnp.float32) + b_two)
    raw_vals = jnp.dot(hid_two, w_three, precision=HIGHEST_MODE, preferred_element_type=jnp.float32)
    envelope = jnp.exp(-positions_f * decay[None, :]) * jnp.sqrt(2.0 * decay + 1.0 / seq_len)[None, :]
    return jnp.transpose(raw_vals * envelope)

def group_pass(items):
    filter_row, query_rows, key_rows, value_rows, cot_rows, bias_vals = items
    fft_len = 2 * LEN
    signal_bf = (key_rows.astype(jnp.float32) * value_rows.astype(jnp.float32)).astype(jnp.bfloat16)
    signal_f = lax.optimization_barrier(signal_bf).astype(jnp.float32)
    filter_spec = jnp.fft.rfft(filter_row.astype(jnp.float32), n=fft_len)
    signal_spec = jnp.fft.rfft(signal_f, n=fft_len, axis=-1)
    conv_part = jnp.fft.irfft(signal_spec * filter_spec[None, :], n=fft_len, axis=-1)[:, :LEN]
    inner_bf = (conv_part + bias_vals[:, None] * signal_f).astype(jnp.bfloat16)
    inner_f = lax.optimization_barrier(inner_bf).astype(jnp.float32)
    query_f = query_rows.astype(jnp.float32)
    cot_f = cot_rows.astype(jnp.float32)
    mixed_rows = (query_f * inner_f).astype(jnp.bfloat16)
    query_grad = (cot_f * inner_f).astype(jnp.bfloat16)
    grad_inner_bf = (cot_f * query_f).astype(jnp.bfloat16)
    grad_inner_f = lax.optimization_barrier(grad_inner_bf).astype(jnp.float32)
    inner_spec = jnp.fft.rfft(grad_inner_f, n=fft_len, axis=-1)
    back_part = jnp.fft.irfft(inner_spec * jnp.conj(filter_spec)[None, :], n=fft_len, axis=-1)[:, :LEN]
    signal_grad = (back_part + bias_vals[:, None] * grad_inner_f).astype(jnp.bfloat16)
    signal_grad_f = lax.optimization_barrier(signal_grad).astype(jnp.float32)
    key_grad = (signal_grad_f * value_rows.astype(jnp.float32)).astype(jnp.bfloat16)
    value_grad = (signal_grad_f * key_rows.astype(jnp.float32)).astype(jnp.bfloat16)
    corr_spec = lax.optimization_barrier(jnp.sum(inner_spec * jnp.conj(signal_spec), axis=0))
    filter_grad = jnp.fft.irfft(corr_spec, n=fft_len)[:LEN].astype(jnp.bfloat16)
    return (mixed_rows, query_grad, key_grad, value_grad, filter_grad)

def grouped_rows(array):
    return array.reshape(GROUPS, GSIZE, LEN)

def reference(query_gate, key_gate, value_in, grad_out, skip_bias, decay, w_first, b_first, w_second, b_second, w_third):
    features, positions_f = position_features(0, LEN, LEN, BANDS)

    def make_filters(w_one, b_one, w_two, b_two, w_three):
        return filter_values(features, positions_f, LEN, decay, w_one, b_one, w_two, b_two, w_three)
    filter_f, pullback = jax.vjp(make_filters, w_first, b_first, w_second, b_second, w_third)
    filters = filter_f.astype(jnp.bfloat16)
    results = lax.map(group_pass, (filters, grouped_rows(query_gate), grouped_rows(key_gate), grouped_rows(value_in), grouped_rows(grad_out), skip_bias.reshape(GROUPS, GSIZE)))
    mixed_out = results[0].reshape(CH, LEN)
    grad_query = results[1].reshape(CH, LEN)
    grad_key = results[2].reshape(CH, LEN)
    grad_value = results[3].reshape(CH, LEN)
    filter_cot = results[4].astype(jnp.float32) * (1.0 / math.sqrt(GSIZE * LEN))
    grad_one, bias_one, grad_two, bias_two, grad_three = pullback(filter_cot)
    return (mixed_out, grad_query, grad_key, grad_value, grad_one, bias_one, grad_two, bias_two, grad_three)
```

```python
import functools
import math

import jax
import jax.numpy as jnp
import ml_dtypes
import numpy as np
from jax import lax
from jax.experimental import pallas as pl
from jax.experimental.pallas import tpu as pltpu
from jax.sharding import PartitionSpec as P

MESH = pl.DeviceIdType.MESH
F32 = jnp.float32
BF16 = jnp.bfloat16
HIGHEST = lax.Precision.HIGHEST

SEQ = 16384
FFT = 2 * SEQ
GSIZE = 16
BANDS = 16
EMB = 2 * BANDS + 1
ORDER = 64
CTX = 16
TP = 8
TOK = SEQ // CTX
CHL = 512
GRL = 32
OWN = CHL // CTX
FROWS = 40
ANY = pl.BlockSpec(memory_space=pl.ANY)
VMEM = pl.BlockSpec(memory_space=pltpu.VMEM)
SMEM = pl.BlockSpec(memory_space=pltpu.SMEM)

PI_A = 3.140625
PI_B = float(np.float32(math.floor((math.pi - PI_A) * 2.0**22) / 2.0**22))
PI_C = math.pi - PI_A - PI_B


def halves(table):
    high = table.astype(ml_dtypes.bfloat16)
    low = (table - high.astype(np.float64)).astype(ml_dtypes.bfloat16)
    return [high, low]


@functools.cache
def tables():
    k1 = np.arange(256)
    n1 = np.arange(128)
    n2 = np.arange(128)
    outer = 2.0 * np.pi * (np.outer(k1, n1) % 256) / 256.0
    cos1, sin1 = np.cos(outer), np.sin(outer)
    by_rows = lambda first, second: np.stack(
        [first.reshape(256, 16, 8), second.reshape(256, 16, 8)], axis=2
    ).reshape(256, 256)
    fwd = np.concatenate([by_rows(cos1, sin1), by_rows(-sin1, cos1)], axis=0)
    inv = np.concatenate([by_rows(cos1, sin1).T, by_rows(-sin1, cos1).T], axis=1) / FFT
    fwd_real = np.concatenate([cos1, -sin1], axis=0)
    inv_real = np.concatenate([cos1.T, -sin1.T], axis=1) / FFT
    inner = 2.0 * np.pi * (np.outer(n2, n2) % 128) / 128.0
    cos2, sin2 = np.cos(inner), np.sin(inner)
    mid_fwd = np.block([[cos2, -sin2], [sin2, cos2]])
    mid_inv = np.block([[cos2, sin2], [-sin2, cos2]])
    turn = 2.0 * np.pi * np.outer(k1, n2) / FFT
    twiddle = np.concatenate([np.cos(turn), -np.sin(turn)], axis=0).astype(np.float32)
    wide = np.concatenate(halves(fwd) + halves(mid_fwd) + halves(mid_inv), axis=0)
    thin = np.concatenate(halves(fwd_real), axis=0)
    long = np.concatenate(halves(inv) + halves(inv_real), axis=0)
    t = np.arange(SEQ, dtype=np.int64)
    steps = np.array([1 + 3 * SEQ // (8 * 2**b) for b in range(BANDS)], dtype=np.int64)
    phase = 2.0 * np.pi * (np.outer(steps, t) % SEQ) / SEQ
    features = np.zeros((FROWS, SEQ), np.float32)
    features[0] = t / SEQ
    features[1 : 1 + BANDS] = np.cos(phase)
    features[1 + BANDS : EMB] = np.sin(phase)
    features[EMB] = 1.0
    return wide, thin, long, twiddle, features


def dot(left, right):
    return jnp.dot(left, right, preferred_element_type=F32)


def dot_full(left, right, dims):
    return lax.dot_general(
        left, right, (dims, ((), ())), precision=HIGHEST, preferred_element_type=F32
    )


def split(x):
    high = x.astype(BF16)
    return high, (x - high.astype(F32)).astype(BF16)


def sin_cos(x):
    turns = jnp.floor(x * (1.0 / math.pi) + 0.5)
    r = ((x - turns * PI_A) - turns * PI_B) - turns * PI_C
    flip = 1.0 - 2.0 * (turns - 2.0 * jnp.floor(turns * 0.5))
    z = r * r
    sine, cosine = 0.0, 0.0
    for i in range(6, -1, -1):
        sine = sine * z + (-1.0) ** i / math.factorial(2 * i + 1)
        cosine = cosine * z + (-1.0) ** i / math.factorial(2 * i)
    return sine * r * flip, cosine * flip


def rows_to_tiles(x):
    return jnp.transpose(jnp.stack([x[:, 128 * i : 128 * i + 128] for i in range(8)], axis=0), (1, 0, 2))


def tiles_to_rows(x):
    x = jnp.transpose(x, (1, 0, 2))
    return jnp.concatenate([x[i] for i in range(8)], axis=1)


S_IN, R_IN, L_IN = 0, 4, 8
S_OUT, R_OUT, L_OUT = 12, 16, 20
S_FIL, R_FIL, S_FG, R_FG, S_RS, R_RS, S_TP, R_TP, S_AG, R_AG = range(24, 34)
C_ARG, C_TAB = 34, 38
N_SEM = 44


def mixer_kernel(
    query, key, value, cot, skip, decay, w1, b1, w2, b2, w3, wide_h, thin_h, long_h, twid_h, feat_h,
    back, summed,
    q_v, k_v, v_v, g_v, wide, thin, long, twid, feat,
    send, recv, spec_s, spec_g, spec_f, corr, out,
    w1a, w2a, h1a, c1, s2, c2, dec, env, fsend, frecv, gsend, grecv, draw, dact, part, rs, tpx, agx, sem,
):
    me = lax.axis_index("ctx")
    tp = lax.axis_index("tp")

    def ring(step):
        return lax.rem(me + step, CTX)

    def remote(src, dst, s, r, axis, j):
        return pltpu.make_async_remote_copy(
            src_ref=src, dst_ref=dst, send_sem=sem.at[s], recv_sem=sem.at[r], device_id={axis: j}, device_id_type=MESH
        )

    def local(src, dst, s):
        return pltpu.make_async_copy(src, dst, sem.at[s])

    def landed(ref, s):
        pltpu.make_async_copy(ref, ref, sem.at[s]).wait()

    loads = [local(a, b, C_ARG + i) for i, (a, b) in enumerate(((key, k_v), (value, v_v), (query, q_v), (cot, g_v)))]
    for c in loads:
        c.start()
    rest = [
        local(feat_h.at[:, pl.ds(pl.multiple_of(me * TOK, TOK), TOK)], feat.at[pl.ds(0, FROWS)], C_TAB),
        local(wide_h, wide, C_TAB + 1),
        local(thin_h, thin, C_TAB + 2),
        local(long_h, long, C_TAB + 3),
        local(twid_h, twid, C_TAB + 4),
    ]
    for c in rest:
        c.start()

    barrier = pltpu.get_barrier_semaphore()

    @pl.loop(1, CTX)
    def _(step):
        pl.semaphore_signal(barrier, inc=1, device_id={"ctx": ring(step)}, device_id_type=MESH)

    @pl.loop(1, TP)
    def _(step):
        pl.semaphore_signal(barrier, inc=1, device_id={"tp": lax.rem(tp + step, TP)}, device_id_type=MESH)

    def product(left, right, j, kind):
        rows = pl.ds(pl.multiple_of(j * OWN, OWN), OWN)
        x = left[rows, :].astype(F32) * right[rows, :].astype(F32)
        y = rows_to_tiles(x).reshape(16, 16, 128).astype(BF16)
        for p in range(16):
            send[2 * kind + p // 8, j, p % 8 // 2, :, 128 * (p % 2) : 128 * (p % 2) + 128] = y[p]

    def mine(rnd):
        return recv.at[rnd, :, pl.ds(pl.multiple_of(me * 16, 16), 16), :]

    def push(rnd, j):
        remote(send.at[rnd, j], mine(rnd), S_IN + rnd, R_IN + rnd, "ctx", j).start()

    loads[0].wait()
    loads[1].wait()
    product(k_v, v_v, me, 0)
    pl.semaphore_wait(barrier, CTX - 1 + TP - 1)

    @pl.loop(1, CTX)
    def _(step):
        product(k_v, v_v, ring(step), 0)
        push(0, ring(step))

    @pl.loop(1, CTX)
    def _(step):
        push(1, ring(step))

    loads[2].wait()
    loads[3].wait()
    product(q_v, g_v, me, 1)

    @pl.loop(1, CTX)
    def _(step):
        product(q_v, g_v, ring(step), 1)
        push(2, ring(step))

    @pl.loop(1, CTX)
    def _(step):
        push(3, ring(step))

    own = [local(send.at[rnd, me], mine(rnd), L_IN + rnd) for rnd in range(4)]
    for c in own:
        c.start()

    rest[0].wait()
    feat[FROWS:, :] = jnp.zeros((64 - FROWS, TOK), F32)
    w1a[...] = jnp.zeros(w1a.shape, F32)
    w1a[0:EMB, :] = w1[...]
    w1a[EMB : EMB + 1, :] = b1[...]
    w2a[...] = jnp.zeros(w2a.shape, F32)
    w2a[0:ORDER, :] = w2[...]
    w2a[ORDER : ORDER + 1, :] = b2[...]
    h1a[ORDER:, :] = (lax.broadcasted_iota(jnp.int32, (8, TOK), 0) == 0).astype(F32)
    sine, cosine = sin_cos(dot_full(w1a[...], feat[0:FROWS, :], ((0,), (0,))))
    h1a[0:ORDER, :] = sine
    c1[...] = cosine
    sine, cosine = sin_cos(dot_full(w2a[...], h1a[...], ((0,), (0,))))
    s2[...] = sine
    c2[...] = cosine
    w3_own = pltpu.roll(w3[...], lax.rem(TP * GRL - tp * GRL, TP * GRL), 1)[:, 0:GRL]
    raw = dot_full(w3_own, s2[...], ((0,), (0,)))
    dec[...] = jnp.zeros(dec.shape, F32)
    dec[0:1, :] = decay[...]
    rate = dot_full(dec[...], h1a[ORDER:, :], ((0,), (0,)))
    position = (me * TOK + lax.broadcasted_iota(jnp.int32, (GRL, TOK), 1)).astype(F32)
    env[...] = jnp.exp(-position * rate) * jnp.sqrt(2.0 * rate + 1.0 / SEQ)
    tiles = rows_to_tiles((raw * env[...]).astype(BF16).astype(F32))
    for j in range(CTX):
        fsend[j, :, 0:128] = tiles[2 * j]
        fsend[j, :, 128:256] = tiles[2 * j + 1]

    @pl.loop(1, CTX)
    def _(step):
        remote(fsend.at[ring(step)], frecv.at[me], S_FIL, R_FIL, "ctx", ring(step)).start()

    frecv[me] = fsend[me]

    for c in rest[1:]:
        c.wait()
    t_re = lambda: twid[0:256, :]
    t_im = lambda: twid[256:512, :]

    def forward_mid(first, pair):
        re = first[0:256, 128 * pair : 128 * pair + 128]
        im = first[256:512, 128 * pair : 128 * pair + 128]
        high, low = split(jnp.concatenate([re * t_re() - im * t_im(), re * t_im() + im * t_re()], axis=1))
        return dot(high, wide[1024:1280, :]) + dot(high, wide[1280:1536, :]) + dot(low, wide[1024:1280, :])

    def inverse_mid(spectra):
        res, ims = [], []
        for spectrum in spectra:
            high, low = split(spectrum)
            x = dot(high, wide[1536:1792, :]) + dot(high, wide[1792:2048, :]) + dot(low, wide[1536:1792, :])
            re, im = x[:, 0:128], x[:, 128:256]
            res.append(re * t_re() + im * t_im())
            ims.append(im * t_re() - re * t_im())
        return split(jnp.concatenate([jnp.concatenate(res, axis=1), jnp.concatenate(ims, axis=1)], axis=0))

    landed(frecv.at[pl.ds(0, CTX - 1)], R_FIL)
    taps = frecv[...].reshape(128, 256).astype(BF16)
    first = dot(thin[0:512, :], taps) + dot(thin[512:1024, :], taps)
    for g in range(2):
        spec_f[g] = forward_mid(first, g)

    def arrived(rnd):
        own[rnd].wait()
        landed(recv.at[rnd, :, pl.ds(0, 240), :], R_IN + rnd)

    def forward(rnd, d, spec, g):
        x = recv[rnd, d]
        first = dot(wide[0:512, :], x) + dot(wide[512:1024, :], x)
        for pair in range(2):
            spec[g, d, pair] = forward_mid(first, pair)

    in_second = lax.broadcasted_iota(jnp.int32, (256, 128), 0) // 8 % 2 == 1

    def inverse(rnd, d, spec, g, sign):
        spectra = []
        for pair in range(2):
            re, im = spec[g, d, pair, :, 0:128], spec[g, d, pair, :, 128:256]
            f_re, f_im = spec_f[g, :, 0:128], sign * spec_f[g, :, 128:256]
            spectra.append(jnp.concatenate([re * f_re - im * f_im, re * f_im + im * f_re], axis=1))
        high, low = inverse_mid(spectra)
        y = dot(long[0:256, :], high) + dot(long[256:512, :], high) + dot(long[0:256, :], low)
        base = me * OWN + g * 16 + d * 4
        scale = jnp.concatenate(
            [jnp.where(in_second, skip[base + 2 * pair + 1], skip[base + 2 * pair]) for pair in range(2)], axis=1
        )
        out[rnd, d] = (y + scale * recv[rnd, d].astype(F32)).astype(BF16)

    def give(rnd):
        @pl.loop(1, CTX)
        def _(step):
            j = ring(step)
            src = out.at[rnd, :, pl.ds(pl.multiple_of(j * 16, 16), 16), :]
            remote(src, back.at[rnd, me], S_OUT + rnd, R_OUT + rnd, "ctx", j).start()

        keep = local(out.at[rnd, :, pl.ds(pl.multiple_of(me * 16, 16), 16), :], back.at[rnd, me], L_OUT + rnd)
        keep.start()
        return keep

    kept = []
    for g in range(2):
        arrived(g)

        @pl.loop(0, 4)
        def _(d):
            forward(g, d, spec_s, g)
            inverse(g, d, spec_s, g, 1.0)

        kept.append(give(g))

    for g in range(2):
        arrived(2 + g)
        corr[g] = jnp.zeros((256, 256), F32)

        @pl.loop(0, 4)
        def _(d):
            forward(2 + g, d, spec_g, g)
            for pair in range(2):
                s_re, s_im = spec_s[g, d, pair, :, 0:128], spec_s[g, d, pair, :, 128:256]
                g_re, g_im = spec_g[g, d, pair, :, 0:128], spec_g[g, d, pair, :, 128:256]
                corr[g, :, 0:128] += g_re * s_re + g_im * s_im
                corr[g, :, 128:256] += g_im * s_re - g_re * s_im

    high, low = inverse_mid([corr[0], corr[1]])
    taps = dot(long[512:640, :], high) + dot(long[640:768, :], high) + dot(long[512:640, :], low)
    gsend[...] = taps.astype(BF16).astype(F32).reshape(CTX, 8, 256)

    @pl.loop(1, CTX)
    def _(step):
        remote(gsend.at[ring(step)], grecv.at[me], S_FG, R_FG, "ctx", ring(step)).start()

    grecv[me] = gsend[me]

    for g in range(2):

        @pl.loop(0, 4)
        def _(d):
            inverse(2 + g, d, spec_g, g, -1.0)

        kept.append(give(2 + g))

    landed(grecv.at[pl.ds(0, CTX - 1)], R_FG)
    got = jnp.stack([grecv[j, :, 128 * g : 128 * g + 128] for j in range(CTX) for g in range(2)], axis=0)
    draw[0:GRL, :] = tiles_to_rows(got) * (1.0 / math.sqrt(GSIZE * SEQ)) * env[...]
    draw[GRL:, :] = jnp.zeros((128 - GRL, TOK), F32)
    w3_own = pltpu.roll(w3[...], lax.rem(TP * GRL - tp * GRL, TP * GRL), 1)[:, 0:GRL]
    dact[0:ORDER, :] = dot_full(w3_own, draw[0:GRL, :], ((1,), (0,))) * c2[...]
    dact[ORDER:, :] = dot_full(w2[...], dact[0:ORDER, :], ((1,), (0,))) * c1[...]
    g_feat = dot_full(feat[...], dact[...], ((1,), (1,)))
    g_hid = dot_full(h1a[0:ORDER, :], dact[...], ((1,), (1,)))
    g_out = dot_full(s2[...], draw[...], ((1,), (1,)))
    g_out = pltpu.roll(jnp.concatenate([g_out, jnp.zeros((ORDER, 128), F32)], axis=1), tp * GRL, 1)
    for i in range(8):
        part[2 * i, :, 0:128] = g_feat[8 * i : 8 * i + 8, :]
        part[2 * i, :, 128:256] = g_hid[8 * i : 8 * i + 8, :]
        part[2 * i + 1] = g_out[8 * i : 8 * i + 8, :]

    @pl.loop(1, CTX)
    def _(step):
        remote(part.at[ring(step)], rs.at[me], S_RS, R_RS, "ctx", ring(step)).start()

    rs[me] = part[me]
    landed(rs.at[pl.ds(0, CTX - 1)], R_RS)
    tpx[tp] = jnp.sum(rs[...], axis=0)

    @pl.loop(1, TP)
    def _(step):
        remote(tpx.at[tp], tpx.at[tp], S_TP, R_TP, "tp", lax.rem(tp + step, TP)).start()

    landed(tpx.at[pl.ds(0, TP - 1)], R_TP)
    agx[me] = jnp.sum(tpx[...], axis=0)

    @pl.loop(1, CTX)
    def _(step):
        remote(agx.at[me], agx.at[me], S_AG, R_AG, "ctx", ring(step)).start()

    landed(agx.at[pl.ds(0, CTX - 1)], R_AG)
    summed[...] = agx[...]

    for rnd in range(4):
        kept[rnd].wait()
        landed(back.at[rnd, pl.ds(0, CTX - 1)], R_OUT + rnd)
    for rnd in range(4):
        landed(send.at[rnd, pl.ds(0, CTX - 1)], S_IN + rnd)
        landed(out.at[rnd, :, pl.ds(0, 240), :], S_OUT + rnd)
    landed(fsend.at[pl.ds(0, CTX - 1)], S_FIL)
    landed(gsend.at[pl.ds(0, CTX - 1)], S_FG)
    landed(part.at[pl.ds(0, CTX - 1)], S_RS)
    landed(tpx.at[pl.ds(0, TP - 1)], S_TP)
    landed(agx.at[pl.ds(0, CTX - 1)], S_AG)


def gate_kernel(
    query, key, value, cot, back, summed, mixed, g_query, g_key, g_value, o_w1, o_b1, o_w2, o_b2, o_w3
):
    count = query.shape[0] // OWN
    for j in range(count):
        rows = slice(OWN * j, OWN * j + OWN)

        def whole(kind):
            tiles = [
                back[2 * kind + p // 8, j, p % 8 // 2, :, 128 * (p % 2) : 128 * (p % 2) + 128] for p in range(16)
            ]
            return tiles_to_rows(jnp.stack(tiles, axis=0).astype(F32).reshape(OWN, 8, 128))

        inner = whole(0)
        mixed[rows, :] = (query[rows, :].astype(F32) * inner).astype(BF16)
        g_query[rows, :] = (cot[rows, :].astype(F32) * inner).astype(BF16)
        g_signal = whole(1)
        g_key[rows, :] = (g_signal * value[rows, :].astype(F32)).astype(BF16)
        g_value[rows, :] = (g_signal * key[rows, :].astype(F32)).astype(BF16)

    @pl.when(pl.program_id(0) == 0)
    def _():
        feat = jnp.concatenate([summed[2 * i, :, 0:128] for i in range(8)], axis=0)
        turned = pltpu.roll(feat, 64, 1)
        o_w1[...] = turned[0:EMB, 0:ORDER]
        o_b1[...] = turned[EMB : EMB + 1, 0:ORDER]
        o_b2[...] = feat[EMB : EMB + 1, 0:ORDER]
        o_w2[...] = jnp.concatenate([summed[2 * i, :, 128:256] for i in range(8)], axis=0)[:, 0:ORDER]
        o_w3[...] = jnp.concatenate([summed[2 * i + 1] for i in range(8)], axis=0)


def on_device(query, key, value, cot, skip, decay, w1, b1, w2, b2, w3):
    wide, thin, long, twid, feat = (jnp.asarray(t) for t in tables())
    f32 = lambda *shape: pltpu.VMEM(shape, F32)
    b16 = lambda *shape: pltpu.VMEM(shape, BF16)
    back, summed = pl.pallas_call(
        mixer_kernel,
        name="mixer",
        out_shape=(
            jax.ShapeDtypeStruct((4, CTX, 4, 16, 256), BF16),
            jax.ShapeDtypeStruct((CTX, 8, 256), F32),
        ),
        in_specs=[ANY] * 4 + [SMEM] + [VMEM] * 6 + [ANY] * 5,
        out_specs=(ANY, VMEM),
        scratch_shapes=[
            *[b16(CHL, TOK) for _ in range(4)],
            b16(*wide.shape), b16(*thin.shape), b16(*long.shape), f32(*twid.shape), f32(64, TOK),
            b16(4, CTX, 4, 16, 256), b16(4, 4, 256, 256),
            f32(2, 4, 2, 256, 256), f32(2, 4, 2, 256, 256), f32(2, 256, 256), f32(2, 256, 256),
            b16(4, 4, 256, 256),
            f32(FROWS, ORDER), f32(ORDER + 8, ORDER), f32(ORDER + 8, TOK), f32(ORDER, TOK), f32(ORDER, TOK),
            f32(ORDER, TOK), f32(8, GRL), f32(GRL, TOK),
            f32(CTX, 8, 256), f32(CTX, 8, 256), f32(CTX, 8, 256), f32(CTX, 8, 256),
            f32(128, TOK), f32(128, TOK),
            f32(CTX, 8, 256), f32(CTX, 8, 256), f32(TP, 8, 256), f32(CTX, 8, 256),
            pltpu.SemaphoreType.DMA((N_SEM,)),
        ],
        compiler_params=pltpu.CompilerParams(
            collective_id=0, has_side_effects=True, vmem_limit_bytes=56 * 1024 * 1024
        ),
        cost_estimate=pl.CostEstimate(flops=12_000_000_000, bytes_accessed=10_000_000, transcendentals=200_000),
    )(query, key, value, cot, skip, decay[None], w1, b1[None], w2, b2[None], w3, wide, thin, long, twid, feat)
    step = 2
    gates = pl.BlockSpec((OWN * step, TOK), lambda i: (i, 0))
    fixed = lambda *shape: pl.BlockSpec(shape, lambda i: (0,) * len(shape))
    mixed, g_query, g_key, g_value, o_w1, o_b1, o_w2, o_b2, o_w3 = pl.pallas_call(
        gate_kernel,
        name="gates",
        grid=(CTX // step,),
        out_shape=tuple(jax.ShapeDtypeStruct((CHL, TOK), BF16) for _ in range(4))
        + tuple(
            jax.ShapeDtypeStruct(s, F32)
            for s in ((EMB, ORDER), (1, ORDER), (ORDER, ORDER), (1, ORDER), (ORDER, TP * GRL))
        ),
        in_specs=[gates] * 4
        + [pl.BlockSpec((4, step, 4, 16, 256), lambda i: (0, i, 0, 0, 0)), fixed(CTX, 8, 256)],
        out_specs=(gates,) * 4
        + (fixed(EMB, ORDER), fixed(1, ORDER), fixed(ORDER, ORDER), fixed(1, ORDER), fixed(ORDER, TP * GRL)),
        compiler_params=pltpu.CompilerParams(vmem_limit_bytes=32 * 1024 * 1024),
        cost_estimate=pl.CostEstimate(flops=4_000_000, bytes_accessed=11_000_000, transcendentals=0),
    )(query, key, value, cot, back, summed)
    return mixed, g_query, g_key, g_value, o_w1, o_b1[0], o_w2, o_b2[0], o_w3


def solution(mesh):
    sharded = P("tp", "ctx")
    return jax.shard_map(
        on_device,
        mesh=mesh,
        in_specs=(sharded,) * 4 + (P("tp"), P("tp")) + (P(),) * 5,
        out_specs=(sharded,) * 4 + (P(),) * 5,
        check_vma=False,
    )
```

```python
import functools
import math

import jax
import jax.numpy as jnp
import ml_dtypes
import numpy as np
from jax import lax
from jax.experimental import pallas as pl
from jax.experimental.pallas import tpu as pltpu
from jax.sharding import PartitionSpec as P

MESH = pl.DeviceIdType.MESH
F32 = jnp.float32
BF16 = jnp.bfloat16
HIGHEST = lax.Precision.HIGHEST

SEQ = 16384
FFT = 2 * SEQ
GSIZE = 16
BANDS = 16
EMB = 2 * BANDS + 1
ORDER = 64
CTX = 16
TP = 8
TOK = SEQ // CTX
CHL = 512
GRL = 32
OWN = CHL // CTX
FROWS = 40
ANY = pl.BlockSpec(memory_space=pl.ANY)
VMEM = pl.BlockSpec(memory_space=pltpu.VMEM)
SMEM = pl.BlockSpec(memory_space=pltpu.SMEM)

PI_A = 3.140625
PI_B = float(np.float32(math.floor((math.pi - PI_A) * 2.0**22) / 2.0**22))
PI_C = math.pi - PI_A - PI_B


def halves(table):
    high = table.astype(ml_dtypes.bfloat16)
    low = (table - high.astype(np.float64)).astype(ml_dtypes.bfloat16)
    return [high, low]


@functools.cache
def tables():
    k1 = np.arange(256)
    n1 = np.arange(128)
    n2 = np.arange(128)
    outer = 2.0 * np.pi * (np.outer(k1, n1) % 256) / 256.0
    cos1, sin1 = np.cos(outer), np.sin(outer)
    by_rows = lambda first, second: np.stack(
        [first.reshape(256, 16, 8), second.reshape(256, 16, 8)], axis=2
    ).reshape(256, 256)
    fwd = np.concatenate([by_rows(cos1, sin1), by_rows(-sin1, cos1)], axis=0)
    inv = np.concatenate([by_rows(cos1, sin1).T, by_rows(-sin1, cos1).T], axis=1) / FFT
    fwd_real = np.concatenate([cos1, -sin1], axis=0)
    inv_real = np.concatenate([cos1.T, -sin1.T], axis=1) / FFT
    inner = 2.0 * np.pi * (np.outer(n2, n2) % 128) / 128.0
    cos2, sin2 = np.cos(inner), np.sin(inner)
    mid_fwd = np.block([[cos2, -sin2], [sin2, cos2]])
    mid_inv = np.block([[cos2, sin2], [-sin2, cos2]])
    turn = 2.0 * np.pi * np.outer(k1, n2) / FFT
    twiddle = np.concatenate([np.cos(turn), -np.sin(turn)], axis=0).astype(np.float32)
    wide = np.concatenate(halves(fwd) + halves(mid_fwd) + halves(mid_inv), axis=0)
    thin = np.concatenate(halves(fwd_real), axis=0)
    long = np.concatenate(halves(inv) + halves(inv_real), axis=0)
    t = np.arange(SEQ, dtype=np.int64)
    steps = np.array([1 + 3 * SEQ // (8 * 2**b) for b in range(BANDS)], dtype=np.int64)
    phase = 2.0 * np.pi * (np.outer(steps, t) % SEQ) / SEQ
    features = np.zeros((FROWS, SEQ), np.float32)
    features[0] = t / SEQ
    features[1 : 1 + BANDS] = np.cos(phase)
    features[1 + BANDS : EMB] = np.sin(phase)
    features[EMB] = 1.0
    return wide, thin, long, twiddle, features


def dot(left, right):
    return jnp.dot(left, right, preferred_element_type=F32)


def dot_full(left, right, dims):
    return lax.dot_general(
        left, right, (dims, ((), ())), precision=HIGHEST, preferred_element_type=F32
    )


def split(x):
    high = x.astype(BF16)
    return high, (x - high.astype(F32)).astype(BF16)


def sin_cos(x):
    turns = jnp.floor(x * (1.0 / math.pi) + 0.5)
    r = ((x - turns * PI_A) - turns * PI_B) - turns * PI_C
    flip = 1.0 - 2.0 * (turns - 2.0 * jnp.floor(turns * 0.5))
    z = r * r
    sine, cosine = 0.0, 0.0
    for i in range(6, -1, -1):
        sine = sine * z + (-1.0) ** i / math.factorial(2 * i + 1)
        cosine = cosine * z + (-1.0) ** i / math.factorial(2 * i)
    return sine * r * flip, cosine * flip


def rows_to_tiles(x):
    return jnp.transpose(jnp.stack([x[:, 128 * i : 128 * i + 128] for i in range(8)], axis=0), (1, 0, 2))


def tiles_to_rows(x):
    x = jnp.transpose(x, (1, 0, 2))
    return jnp.concatenate([x[i] for i in range(8)], axis=1)


S_IN, R_IN, L_IN = 0, 4, 8
S_OUT, R_OUT, L_OUT = 12, 16, 20
S_FIL, R_FIL, S_FG, R_FG, S_RS, R_RS, S_TP, R_TP, S_AG, R_AG = range(24, 34)
C_ARG, C_TAB = 34, 38
N_SEM = 44


def mixer_kernel(
    query, key, value, cot, skip, decay, w1, b1, w2, b2, w3, wide_h, thin_h, long_h, twid_h, feat_h,
    back, summed,
    q_v, k_v, v_v, g_v, wide, thin, long, twid, feat,
    send, recv, spec_s, spec_g, spec_f, corr, out,
    w1a, w2a, h1a, c1, s2, c2, dec, env, fsend, frecv, gsend, grecv, draw, dact, part, rs, tpx, agx, sem,
):
    me = lax.axis_index("ctx")
    tp = lax.axis_index("tp")

    def ring(step):
        return lax.rem(me + step, CTX)

    def remote(src, dst, s, r, axis, j):
        return pltpu.make_async_remote_copy(
            src_ref=src, dst_ref=dst, send_sem=sem.at[s], recv_sem=sem.at[r], device_id={axis: j}, device_id_type=MESH
        )

    def local(src, dst, s):
        return pltpu.make_async_copy(src, dst, sem.at[s])

    def landed(ref, s):
        pltpu.make_async_copy(ref, ref, sem.at[s]).wait()

    loads = [local(a, b, C_ARG + i) for i, (a, b) in enumerate(((key, k_v), (value, v_v), (query, q_v), (cot, g_v)))]
    for c in loads:
        c.start()
    rest = [
        local(feat_h.at[:, pl.ds(pl.multiple_of(me * TOK, TOK), TOK)], feat.at[pl.ds(0, FROWS)], C_TAB),
        local(wide_h, wide, C_TAB + 1),
        local(thin_h, thin, C_TAB + 2),
        local(long_h, long, C_TAB + 3),
        local(twid_h, twid, C_TAB + 4),
    ]
    for c in rest:
        c.start()

    barrier = pltpu.get_barrier_semaphore()

    @pl.loop(1, CTX)
    def _(step):
        pl.semaphore_signal(barrier, inc=1, device_id={"ctx": ring(step)}, device_id_type=MESH)

    @pl.loop(1, TP)
    def _(step):
        pl.semaphore_signal(barrier, inc=1, device_id={"tp": lax.rem(tp + step, TP)}, device_id_type=MESH)

    def product(left, right, j, kind):
        rows = pl.ds(pl.multiple_of(j * OWN, OWN), OWN)
        x = left[rows, :].astype(F32) * right[rows, :].astype(F32)
        y = rows_to_tiles(x).reshape(16, 16, 128).astype(BF16)
        for p in range(16):
            send[2 * kind + p // 8, j, p % 8 // 2, :, 128 * (p % 2) : 128 * (p % 2) + 128] = y[p]

    def mine(rnd):
        return recv.at[rnd, :, pl.ds(pl.multiple_of(me * 16, 16), 16), :]

    def push(rnd, j):
        remote(send.at[rnd, j], mine(rnd), S_IN + rnd, R_IN + rnd, "ctx", j).start()

    def push_all(rnd):
        @pl.loop(1, CTX)
        def _(step):
            push(rnd, ring(step))

    loads[0].wait()
    loads[1].wait()
    product(k_v, v_v, me, 0)
    pl.semaphore_wait(barrier, CTX - 1 + TP - 1)

    @pl.loop(1, CTX)
    def _(step):
        product(k_v, v_v, ring(step), 0)
        push(0, ring(step))

    loads[2].wait()
    loads[3].wait()

    @pl.loop(0, CTX)
    def _(j):
        product(q_v, g_v, j, 1)

    own = [local(send.at[rnd, me], mine(rnd), L_IN + rnd) for rnd in range(4)]
    for c in own:
        c.start()

    rest[0].wait()
    feat[FROWS:, :] = jnp.zeros((64 - FROWS, TOK), F32)
    w1a[...] = jnp.zeros(w1a.shape, F32)
    w1a[0:EMB, :] = w1[...]
    w1a[EMB : EMB + 1, :] = b1[...]
    w2a[...] = jnp.zeros(w2a.shape, F32)
    w2a[0:ORDER, :] = w2[...]
    w2a[ORDER : ORDER + 1, :] = b2[...]
    h1a[ORDER:, :] = (lax.broadcasted_iota(jnp.int32, (8, TOK), 0) == 0).astype(F32)
    sine, cosine = sin_cos(dot_full(w1a[...], feat[0:FROWS, :], ((0,), (0,))))
    h1a[0:ORDER, :] = sine
    c1[...] = cosine
    sine, cosine = sin_cos(dot_full(w2a[...], h1a[...], ((0,), (0,))))
    s2[...] = sine
    c2[...] = cosine
    w3_own = pltpu.roll(w3[...], lax.rem(TP * GRL - tp * GRL, TP * GRL), 1)[:, 0:GRL]
    raw = dot_full(w3_own, s2[...], ((0,), (0,)))
    dec[...] = jnp.zeros(dec.shape, F32)
    dec[0:1, :] = decay[...]
    rate = dot_full(dec[...], h1a[ORDER:, :], ((0,), (0,)))
    position = (me * TOK + lax.broadcasted_iota(jnp.int32, (GRL, TOK), 1)).astype(F32)
    env[...] = jnp.exp(-position * rate) * jnp.sqrt(2.0 * rate + 1.0 / SEQ)
    tiles = rows_to_tiles((raw * env[...]).astype(BF16).astype(F32))
    for j in range(CTX):
        fsend[j, :, 0:128] = tiles[2 * j]
        fsend[j, :, 128:256] = tiles[2 * j + 1]

    @pl.loop(1, CTX)
    def _(step):
        remote(fsend.at[ring(step)], frecv.at[me], S_FIL, R_FIL, "ctx", ring(step)).start()

    frecv[me] = fsend[me]
    push_all(2)

    for c in rest[1:]:
        c.wait()
    t_re = lambda: twid[0:256, :]
    t_im = lambda: twid[256:512, :]

    def forward_mid(first, pair):
        re = first[0:256, 128 * pair : 128 * pair + 128]
        im = first[256:512, 128 * pair : 128 * pair + 128]
        high, low = split(jnp.concatenate([re * t_re() - im * t_im(), re * t_im() + im * t_re()], axis=1))
        return dot(high, wide[1024:1280, :]) + dot(high, wide[1280:1536, :]) + dot(low, wide[1024:1280, :])

    def inverse_mid(spectra):
        res, ims = [], []
        for spectrum in spectra:
            high, low = split(spectrum)
            x = dot(high, wide[1536:1792, :]) + dot(high, wide[1792:2048, :]) + dot(low, wide[1536:1792, :])
            re, im = x[:, 0:128], x[:, 128:256]
            res.append(re * t_re() + im * t_im())
            ims.append(im * t_re() - re * t_im())
        return split(jnp.concatenate([jnp.concatenate(res, axis=1), jnp.concatenate(ims, axis=1)], axis=0))

    landed(frecv.at[pl.ds(0, CTX - 1)], R_FIL)
    taps = frecv[...].reshape(128, 256).astype(BF16)
    first = dot(thin[0:512, :], taps) + dot(thin[512:1024, :], taps)
    for g in range(2):
        spec_f[g] = forward_mid(first, g)

    def arrived(rnd):
        own[rnd].wait()
        landed(recv.at[rnd, :, pl.ds(0, 240), :], R_IN + rnd)

    def forward(rnd, d, spec, g):
        x = recv[rnd, d]
        first = dot(wide[0:512, :], x) + dot(wide[512:1024, :], x)
        for pair in range(2):
            spec[g, d, pair] = forward_mid(first, pair)

    in_second = lax.broadcasted_iota(jnp.int32, (256, 128), 0) // 8 % 2 == 1

    def inverse(rnd, d, spec, g, sign):
        spectra = []
        for pair in range(2):
            re, im = spec[g, d, pair, :, 0:128], spec[g, d, pair, :, 128:256]
            f_re, f_im = spec_f[g, :, 0:128], sign * spec_f[g, :, 128:256]
            spectra.append(jnp.concatenate([re * f_re - im * f_im, re * f_im + im * f_re], axis=1))
        high, low = inverse_mid(spectra)
        y = dot(long[0:256, :], high) + dot(long[256:512, :], high) + dot(long[0:256, :], low)
        base = me * OWN + g * 16 + d * 4
        scale = jnp.concatenate(
            [jnp.where(in_second, skip[base + 2 * pair + 1], skip[base + 2 * pair]) for pair in range(2)], axis=1
        )
        out[rnd, d] = (y + scale * recv[rnd, d].astype(F32)).astype(BF16)

    def give(rnd):
        @pl.loop(1, CTX)
        def _(step):
            j = ring(step)
            src = out.at[rnd, :, pl.ds(pl.multiple_of(j * 16, 16), 16), :]
            remote(src, back.at[rnd, me], S_OUT + rnd, R_OUT + rnd, "ctx", j).start()

        keep = local(out.at[rnd, :, pl.ds(pl.multiple_of(me * 16, 16), 16), :], back.at[rnd, me], L_OUT + rnd)
        keep.start()
        return keep

    def each_duo(*steps):
        @pl.loop(0, 4)
        def _(d):
            for step in steps:
                step(d)

    def forward_signal(g):
        return lambda d: forward(g, d, spec_s, g)

    def inverse_signal(g):
        return lambda d: inverse(g, d, spec_s, g, 1.0)

    def inverse_grad(g):
        return lambda d: inverse(2 + g, d, spec_g, g, -1.0)

    def forward_grad(g):
        corr[g] = jnp.zeros((256, 256), F32)

        def step(d):
            forward(2 + g, d, spec_g, g)
            for pair in range(2):
                s_re, s_im = spec_s[g, d, pair, :, 0:128], spec_s[g, d, pair, :, 128:256]
                g_re, g_im = spec_g[g, d, pair, :, 0:128], spec_g[g, d, pair, :, 128:256]
                corr[g, :, 0:128] += g_re * s_re + g_im * s_im
                corr[g, :, 128:256] += g_im * s_re - g_re * s_im

        return step

    arrived(0)
    push_all(1)
    each_duo(forward_signal(0), inverse_signal(0))
    push_all(3)
    kept = [give(0)]
    arrived(2)
    each_duo(forward_grad(0), inverse_grad(0))
    kept.append(give(2))
    arrived(1)
    each_duo(forward_signal(1))
    arrived(3)
    each_duo(forward_grad(1))

    high, low = inverse_mid([corr[0], corr[1]])
    taps = dot(long[512:640, :], high) + dot(long[640:768, :], high) + dot(long[512:640, :], low)
    gsend[...] = taps.astype(BF16).astype(F32).reshape(CTX, 8, 256)

    @pl.loop(1, CTX)
    def _(step):
        remote(gsend.at[ring(step)], grecv.at[me], S_FG, R_FG, "ctx", ring(step)).start()

    grecv[me] = gsend[me]
    each_duo(inverse_signal(1))
    kept.append(give(1))

    landed(grecv.at[pl.ds(0, CTX - 1)], R_FG)
    got = jnp.stack([grecv[j, :, 128 * g : 128 * g + 128] for j in range(CTX) for g in range(2)], axis=0)
    draw[0:GRL, :] = tiles_to_rows(got) * (1.0 / math.sqrt(GSIZE * SEQ)) * env[...]
    draw[GRL:, :] = jnp.zeros((128 - GRL, TOK), F32)
    w3_own = pltpu.roll(w3[...], lax.rem(TP * GRL - tp * GRL, TP * GRL), 1)[:, 0:GRL]
    dact[0:ORDER, :] = dot_full(w3_own, draw[0:GRL, :], ((1,), (0,))) * c2[...]
    dact[ORDER:, :] = dot_full(w2[...], dact[0:ORDER, :], ((1,), (0,))) * c1[...]
    g_feat = dot_full(feat[...], dact[...], ((1,), (1,)))
    g_hid = dot_full(h1a[0:ORDER, :], dact[...], ((1,), (1,)))
    g_out = dot_full(s2[...], draw[...], ((1,), (1,)))
    g_out = pltpu.roll(jnp.concatenate([g_out, jnp.zeros((ORDER, 128), F32)], axis=1), tp * GRL, 1)
    for i in range(8):
        part[2 * i, :, 0:128] = g_feat[8 * i : 8 * i + 8, :]
        part[2 * i, :, 128:256] = g_hid[8 * i : 8 * i + 8, :]
        part[2 * i + 1] = g_out[8 * i : 8 * i + 8, :]

    @pl.loop(1, CTX)
    def _(step):
        remote(part.at[ring(step)], rs.at[me], S_RS, R_RS, "ctx", ring(step)).start()

    rs[me] = part[me]
    each_duo(inverse_grad(1))
    kept.append(give(3))
    landed(rs.at[pl.ds(0, CTX - 1)], R_RS)
    tpx[tp] = jnp.sum(rs[...], axis=0)

    @pl.loop(1, TP)
    def _(step):
        remote(tpx.at[tp], tpx.at[tp], S_TP, R_TP, "tp", lax.rem(tp + step, TP)).start()

    landed(tpx.at[pl.ds(0, TP - 1)], R_TP)
    agx[me] = jnp.sum(tpx[...], axis=0)

    @pl.loop(1, CTX)
    def _(step):
        remote(agx.at[me], agx.at[me], S_AG, R_AG, "ctx", ring(step)).start()

    landed(agx.at[pl.ds(0, CTX - 1)], R_AG)
    summed[...] = agx[...]

    for c in kept:
        c.wait()
    for rnd in range(4):
        landed(back.at[rnd, pl.ds(0, CTX - 1)], R_OUT + rnd)
    for rnd in range(4):
        landed(send.at[rnd, pl.ds(0, CTX - 1)], S_IN + rnd)
        landed(out.at[rnd, :, pl.ds(0, 240), :], S_OUT + rnd)
    landed(fsend.at[pl.ds(0, CTX - 1)], S_FIL)
    landed(gsend.at[pl.ds(0, CTX - 1)], S_FG)
    landed(part.at[pl.ds(0, CTX - 1)], S_RS)
    landed(tpx.at[pl.ds(0, TP - 1)], S_TP)
    landed(agx.at[pl.ds(0, CTX - 1)], S_AG)


def gate_kernel(
    query, key, value, cot, back, summed, mixed, g_query, g_key, g_value, o_w1, o_b1, o_w2, o_b2, o_w3
):
    count = query.shape[0] // OWN
    for j in range(count):
        rows = slice(OWN * j, OWN * j + OWN)

        def whole(kind):
            tiles = [
                back[2 * kind + p // 8, j, p % 8 // 2, :, 128 * (p % 2) : 128 * (p % 2) + 128] for p in range(16)
            ]
            return tiles_to_rows(jnp.stack(tiles, axis=0).astype(F32).reshape(OWN, 8, 128))

        inner = whole(0)
        mixed[rows, :] = (query[rows, :].astype(F32) * inner).astype(BF16)
        g_query[rows, :] = (cot[rows, :].astype(F32) * inner).astype(BF16)
        g_signal = whole(1)
        g_key[rows, :] = (g_signal * value[rows, :].astype(F32)).astype(BF16)
        g_value[rows, :] = (g_signal * key[rows, :].astype(F32)).astype(BF16)

    @pl.when(pl.program_id(0) == 0)
    def _():
        feat = jnp.concatenate([summed[2 * i, :, 0:128] for i in range(8)], axis=0)
        turned = pltpu.roll(feat, 64, 1)
        o_w1[...] = turned[0:EMB, 0:ORDER]
        o_b1[...] = turned[EMB : EMB + 1, 0:ORDER]
        o_b2[...] = feat[EMB : EMB + 1, 0:ORDER]
        o_w2[...] = jnp.concatenate([summed[2 * i, :, 128:256] for i in range(8)], axis=0)[:, 0:ORDER]
        o_w3[...] = jnp.concatenate([summed[2 * i + 1] for i in range(8)], axis=0)


def on_device(query, key, value, cot, skip, decay, w1, b1, w2, b2, w3):
    wide, thin, long, twid, feat = (jnp.asarray(t) for t in tables())
    f32 = lambda *shape: pltpu.VMEM(shape, F32)
    b16 = lambda *shape: pltpu.VMEM(shape, BF16)
    back, summed = pl.pallas_call(
        mixer_kernel,
        name="mixer",
        out_shape=(
            jax.ShapeDtypeStruct((4, CTX, 4, 16, 256), BF16),
            jax.ShapeDtypeStruct((CTX, 8, 256), F32),
        ),
        in_specs=[ANY] * 4 + [SMEM] + [VMEM] * 6 + [ANY] * 5,
        out_specs=(ANY, VMEM),
        scratch_shapes=[
            *[b16(CHL, TOK) for _ in range(4)],
            b16(*wide.shape), b16(*thin.shape), b16(*long.shape), f32(*twid.shape), f32(64, TOK),
            b16(4, CTX, 4, 16, 256), b16(4, 4, 256, 256),
            f32(2, 4, 2, 256, 256), f32(2, 4, 2, 256, 256), f32(2, 256, 256), f32(2, 256, 256),
            b16(4, 4, 256, 256),
            f32(FROWS, ORDER), f32(ORDER + 8, ORDER), f32(ORDER + 8, TOK), f32(ORDER, TOK), f32(ORDER, TOK),
            f32(ORDER, TOK), f32(8, GRL), f32(GRL, TOK),
            f32(CTX, 8, 256), f32(CTX, 8, 256), f32(CTX, 8, 256), f32(CTX, 8, 256),
            f32(128, TOK), f32(128, TOK),
            f32(CTX, 8, 256), f32(CTX, 8, 256), f32(TP, 8, 256), f32(CTX, 8, 256),
            pltpu.SemaphoreType.DMA((N_SEM,)),
        ],
        compiler_params=pltpu.CompilerParams(
            collective_id=0, has_side_effects=True, vmem_limit_bytes=56 * 1024 * 1024
        ),
        cost_estimate=pl.CostEstimate(flops=12_000_000_000, bytes_accessed=10_000_000, transcendentals=200_000),
    )(query, key, value, cot, skip, decay[None], w1, b1[None], w2, b2[None], w3, wide, thin, long, twid, feat)
    step = 2
    gates = pl.BlockSpec((OWN * step, TOK), lambda i: (i, 0))
    fixed = lambda *shape: pl.BlockSpec(shape, lambda i: (0,) * len(shape))
    mixed, g_query, g_key, g_value, o_w1, o_b1, o_w2, o_b2, o_w3 = pl.pallas_call(
        gate_kernel,
        name="gates",
        grid=(CTX // step,),
        out_shape=tuple(jax.ShapeDtypeStruct((CHL, TOK), BF16) for _ in range(4))
        + tuple(
            jax.ShapeDtypeStruct(s, F32)
            for s in ((EMB, ORDER), (1, ORDER), (ORDER, ORDER), (1, ORDER), (ORDER, TP * GRL))
        ),
        in_specs=[gates] * 4
        + [pl.BlockSpec((4, step, 4, 16, 256), lambda i: (0, i, 0, 0, 0)), fixed(CTX, 8, 256)],
        out_specs=(gates,) * 4
        + (fixed(EMB, ORDER), fixed(1, ORDER), fixed(ORDER, ORDER), fixed(1, ORDER), fixed(ORDER, TP * GRL)),
        compiler_params=pltpu.CompilerParams(vmem_limit_bytes=32 * 1024 * 1024),
        cost_estimate=pl.CostEstimate(flops=4_000_000, bytes_accessed=11_000_000, transcendentals=0),
    )(query, key, value, cot, back, summed)
    return mixed, g_query, g_key, g_value, o_w1, o_b1[0], o_w2, o_b2[0], o_w3


def solution(mesh):
    sharded = P("tp", "ctx")
    return jax.shard_map(
        on_device,
        mesh=mesh,
        in_specs=(sharded,) * 4 + (P("tp"), P("tp")) + (P(),) * 5,
        out_specs=(sharded,) * 4 + (P(),) * 5,
        check_vma=False,
    )
```

```python
import functools
import math

import jax
import jax.numpy as jnp
import ml_dtypes
import numpy as np
from jax import lax
from jax.experimental import pallas as pl
from jax.experimental.pallas import tpu as pltpu
from jax.sharding import PartitionSpec as P

MESH = pl.DeviceIdType.MESH
F32 = jnp.float32
BF16 = jnp.bfloat16
HIGHEST = lax.Precision.HIGHEST

SEQ = 16384
FFT = 2 * SEQ
GSIZE = 16
BANDS = 16
EMB = 2 * BANDS + 1
ORDER = 64
CTX = 16
TP = 8
TOK = SEQ // CTX
CHL = 512
GRL = 32
OWN = CHL // CTX
FROWS = 40
ANY = pl.BlockSpec(memory_space=pl.ANY)
VMEM = pl.BlockSpec(memory_space=pltpu.VMEM)
SMEM = pl.BlockSpec(memory_space=pltpu.SMEM)
HBM = pl.BlockSpec(memory_space=pltpu.HBM)

PI_A = 3.140625
PI_B = float(np.float32(math.floor((math.pi - PI_A) * 2.0**22) / 2.0**22))
PI_C = math.pi - PI_A - PI_B


def halves(table):
    high = table.astype(ml_dtypes.bfloat16)
    low = (table - high.astype(np.float64)).astype(ml_dtypes.bfloat16)
    return [high, low]


@functools.cache
def tables():
    k1 = np.arange(256)
    n1 = np.arange(128)
    n2 = np.arange(128)
    outer = 2.0 * np.pi * (np.outer(k1, n1) % 256) / 256.0
    cos1, sin1 = np.cos(outer), np.sin(outer)
    by_rows = lambda first, second: np.stack(
        [first.reshape(256, 16, 8), second.reshape(256, 16, 8)], axis=2
    ).reshape(256, 256)
    fwd = np.concatenate([by_rows(cos1, sin1), by_rows(-sin1, cos1)], axis=0)
    inv = np.concatenate([by_rows(cos1, sin1).T, by_rows(-sin1, cos1).T], axis=1) / FFT
    fwd_real = np.concatenate([cos1, -sin1], axis=0)
    inv_real = np.concatenate([cos1.T, -sin1.T], axis=1) / FFT
    inner = 2.0 * np.pi * (np.outer(n2, n2) % 128) / 128.0
    cos2, sin2 = np.cos(inner), np.sin(inner)
    mid_fwd = np.block([[cos2, -sin2], [sin2, cos2]])
    mid_inv = np.block([[cos2, sin2], [-sin2, cos2]])
    turn = 2.0 * np.pi * np.outer(k1, n2) / FFT
    twiddle = np.concatenate([np.cos(turn), -np.sin(turn)], axis=0).astype(np.float32)
    wide = np.concatenate(halves(fwd) + halves(mid_fwd) + halves(mid_inv), axis=0)
    thin = np.concatenate(halves(fwd_real), axis=0)
    long = np.concatenate(halves(inv) + halves(inv_real), axis=0)
    t = np.arange(SEQ, dtype=np.int64)
    steps = np.array([1 + 3 * SEQ // (8 * 2**b) for b in range(BANDS)], dtype=np.int64)
    phase = 2.0 * np.pi * (np.outer(steps, t) % SEQ) / SEQ
    features = np.zeros((FROWS, SEQ), np.float32)
    features[0] = t / SEQ
    features[1 : 1 + BANDS] = np.cos(phase)
    features[1 + BANDS : EMB] = np.sin(phase)
    features[EMB] = 1.0
    return wide, thin, long, twiddle, features


def dot(left, right):
    return jnp.dot(left, right, preferred_element_type=F32)


def dot_full(left, right, dims):
    return lax.dot_general(
        left, right, (dims, ((), ())), precision=HIGHEST, preferred_element_type=F32
    )


def split(x):
    high = x.astype(BF16)
    return high, (x - high.astype(F32)).astype(BF16)


def sin_cos(x):
    turns = jnp.floor(x * (1.0 / math.pi) + 0.5)
    r = ((x - turns * PI_A) - turns * PI_B) - turns * PI_C
    flip = 1.0 - 2.0 * (turns - 2.0 * jnp.floor(turns * 0.5))
    z = r * r
    sine, cosine = 0.0, 0.0
    for i in range(6, -1, -1):
        sine = sine * z + (-1.0) ** i / math.factorial(2 * i + 1)
        cosine = cosine * z + (-1.0) ** i / math.factorial(2 * i)
    return sine * r * flip, cosine * flip


def rows_to_tiles(x):
    return jnp.transpose(jnp.stack([x[:, 128 * i : 128 * i + 128] for i in range(8)], axis=0), (1, 0, 2))


def tiles_to_rows(x):
    x = jnp.transpose(x, (1, 0, 2))
    return jnp.concatenate([x[i] for i in range(8)], axis=1)


S_IN, R_IN, L_IN = 0, 4, 8
S_OUT, R_OUT, L_OUT = 12, 16, 20
S_FIL, R_FIL, S_FG, R_FG, S_RS, R_RS, S_TP, R_TP, S_AG, R_AG = range(24, 34)
C_ARG, C_TAB, C_SMALL = 34, 38, 43
N_SEM = 49


def mixer_kernel(
    query, key, value, cot, skip, decay_h, w1_h, b1_h, w2_h, b2_h, w3_h, wide_h, thin_h, long_h, twid_h, feat_h,
    back, summed,
    q_v, k_v, v_v, g_v, decay, w1, b1, w2, b2, w3, wide, thin, long, twid, feat,
    send, recv, spec_s, spec_g, spec_f, corr, rows_f, out,
    w1a, w2a, h1a, c1, s2, c2, dec, env, fsend, frecv, gsend, grecv, draw, dact, m_feat, m_out, part, rs, tpx, agx, sem,
):
    me = lax.axis_index("ctx")
    tp = lax.axis_index("tp")

    def ring(step):
        return lax.rem(me + step, CTX)

    barrier = pltpu.get_barrier_semaphore()

    @pl.loop(1, CTX)
    def _(step):
        pl.semaphore_signal(barrier, inc=1, device_id={"ctx": ring(step)}, device_id_type=MESH)

    @pl.loop(1, TP)
    def _(step):
        pl.semaphore_signal(barrier, inc=1, device_id={"tp": lax.rem(tp + step, TP)}, device_id_type=MESH)

    def remote(src, dst, s, r, axis, j):
        return pltpu.make_async_remote_copy(
            src_ref=src, dst_ref=dst, send_sem=sem.at[s], recv_sem=sem.at[r], device_id={axis: j}, device_id_type=MESH
        )

    def local(src, dst, s):
        return pltpu.make_async_copy(src, dst, sem.at[s])

    def landed(ref, s):
        pltpu.make_async_copy(ref, ref, sem.at[s]).wait()

    loads = [local(a, b, C_ARG + i) for i, (a, b) in enumerate(((key, k_v), (value, v_v), (query, q_v), (cot, g_v)))]
    for c in loads:
        c.start()
    rest = [
        local(feat_h.at[:, pl.ds(pl.multiple_of(me * TOK, TOK), TOK)], feat.at[pl.ds(0, FROWS)], C_TAB),
        local(wide_h, wide, C_TAB + 1),
        local(thin_h, thin, C_TAB + 2),
        local(long_h, long, C_TAB + 3),
        local(twid_h, twid, C_TAB + 4),
    ]
    small = [
        local(a, b, C_SMALL + i)
        for i, (a, b) in enumerate(
            ((decay_h, decay), (w1_h, w1), (b1_h, b1), (w2_h, w2), (b2_h, b2), (w3_h, w3))
        )
    ]
    for c in rest[:1] + small + rest[1:]:
        c.start()

    def product(left, right, j, kind):
        rows = pl.ds(pl.multiple_of(j * OWN, OWN), OWN)
        x = left[rows, :].astype(F32) * right[rows, :].astype(F32)
        y = rows_to_tiles(x).reshape(16, 16, 128).astype(BF16)
        for p in range(16):
            send[2 * kind + p // 8, j, p % 8 // 2, :, 128 * (p % 2) : 128 * (p % 2) + 128] = y[p]

    def mine(rnd):
        return recv.at[rnd, :, pl.ds(pl.multiple_of(me * 16, 16), 16), :]

    def push(rnd, j):
        remote(send.at[rnd, j], mine(rnd), S_IN + rnd, R_IN + rnd, "ctx", j).start()

    def push_all(rnd):
        @pl.loop(1, CTX)
        def _(step):
            push(rnd, ring(step))

    loads[0].wait()
    loads[1].wait()
    product(k_v, v_v, me, 0)
    pl.semaphore_wait(barrier, CTX - 1 + TP - 1)

    @pl.loop(1, CTX)
    def _(step):
        product(k_v, v_v, ring(step), 0)
        push(0, ring(step))

    loads[2].wait()
    loads[3].wait()

    @pl.loop(0, CTX)
    def _(j):
        product(q_v, g_v, j, 1)

    push_all(2)
    own = [local(send.at[rnd, me], mine(rnd), L_IN + rnd) for rnd in range(4)]
    for c in own:
        c.start()

    rest[0].wait()
    for c in small:
        c.wait()
    feat[FROWS:, :] = jnp.zeros((64 - FROWS, TOK), F32)
    w1a[...] = jnp.zeros(w1a.shape, F32)
    w1a[0:EMB, :] = w1[...]
    w1a[EMB : EMB + 1, :] = b1[...]
    w2a[...] = jnp.zeros(w2a.shape, F32)
    w2a[0:ORDER, :] = w2[...]
    w2a[ORDER : ORDER + 1, :] = b2[...]
    h1a[ORDER:, :] = (lax.broadcasted_iota(jnp.int32, (8, TOK), 0) == 0).astype(F32)
    sine, cosine = sin_cos(dot_full(w1a[...], feat[0:FROWS, :], ((0,), (0,))))
    h1a[0:ORDER, :] = sine
    c1[...] = cosine
    sine, cosine = sin_cos(dot_full(w2a[...], h1a[...], ((0,), (0,))))
    s2[...] = sine
    c2[...] = cosine
    w3_own = pltpu.roll(w3[...], lax.rem(TP * GRL - tp * GRL, TP * GRL), 1)[:, 0:GRL]
    raw = dot_full(w3_own, s2[...], ((0,), (0,)))
    dec[...] = jnp.zeros(dec.shape, F32)
    dec[0:1, :] = decay[...]
    rate = dot_full(dec[...], h1a[ORDER:, :], ((0,), (0,)))
    position = (me * TOK + lax.broadcasted_iota(jnp.int32, (GRL, TOK), 1)).astype(F32)
    env[...] = jnp.exp(-position * rate) * jnp.sqrt(2.0 * rate + 1.0 / SEQ)
    fsend[...] = rows_to_tiles(raw * env[...]).reshape(CTX, 16, 128).astype(BF16)

    @pl.loop(1, CTX)
    def _(step):
        remote(fsend.at[ring(step)], frecv.at[me], S_FIL, R_FIL, "ctx", ring(step)).start()

    frecv[me] = fsend[me]
    push_all(1)

    for c in rest[1:]:
        c.wait()
    t_re = lambda: twid[0:256, :]
    t_im = lambda: twid[256:512, :]

    def forward_mid(first, pair):
        re = first[0:256, 128 * pair : 128 * pair + 128]
        im = first[256:512, 128 * pair : 128 * pair + 128]
        high, low = split(jnp.concatenate([re * t_re() - im * t_im(), re * t_im() + im * t_re()], axis=1))
        return dot(high, wide[1024:1280, :]) + dot(high, wide[1280:1536, :]) + dot(low, wide[1024:1280, :])

    def inverse_mid(spectra):
        res, ims = [], []
        for spectrum in spectra:
            high, low = split(spectrum)
            x = dot(high, wide[1536:1792, :]) + dot(high, wide[1792:2048, :]) + dot(low, wide[1536:1792, :])
            re, im = x[:, 0:128], x[:, 128:256]
            res.append(re * t_re() + im * t_im())
            ims.append(im * t_re() - re * t_im())
        return split(jnp.concatenate([jnp.concatenate(res, axis=1), jnp.concatenate(ims, axis=1)], axis=0))

    landed(frecv.at[pl.ds(0, CTX - 1)], R_FIL)
    taps = frecv[...].astype(F32).reshape(CTX, 2, 8, 128)
    taps = jnp.concatenate([taps[:, g].reshape(128, 128) for g in range(2)], axis=1).astype(BF16)
    first = dot(thin[0:512, :], taps) + dot(thin[512:1024, :], taps)
    for g in range(2):
        spec_f[g] = forward_mid(first, g)

    def arrived(rnd):
        own[rnd].wait()
        landed(recv.at[rnd, :, pl.ds(0, 240), :], R_IN + rnd)

    def forward(rnd, d, spec, g):
        x = recv[rnd, d]
        first = dot(wide[0:512, :], x) + dot(wide[512:1024, :], x)
        for pair in range(2):
            spec[g, d, pair] = forward_mid(first, pair)

    in_second = lax.broadcasted_iota(jnp.int32, (256, 128), 0) // 8 % 2 == 1

    def inverse(rnd, d, spec, g, sign):
        spectra = []
        for pair in range(2):
            re, im = spec[g, d, pair, :, 0:128], spec[g, d, pair, :, 128:256]
            f_re, f_im = spec_f[g, :, 0:128], sign * spec_f[g, :, 128:256]
            spectra.append(jnp.concatenate([re * f_re - im * f_im, re * f_im + im * f_re], axis=1))
        high, low = inverse_mid(spectra)
        y = dot(long[0:256, :], high) + dot(long[256:512, :], high) + dot(long[0:256, :], low)
        base = me * OWN + g * 16 + d * 4
        scale = jnp.concatenate(
            [jnp.where(in_second, skip[base + 2 * pair + 1], skip[base + 2 * pair]) for pair in range(2)], axis=1
        )
        rows_f[d] = y + scale * recv[rnd, d].astype(F32)

    def back_rows(rnd):
        return back.at[rnd // 2, pl.ds(pl.multiple_of(me * OWN + rnd % 2 * 16, 16), 16), :]

    def give(rnd):
        def turn(j):
            block = pl.ds(pl.multiple_of(j * 16, 16), 16)
            tiles = [rows_f[d, block, 128 * p : 128 * p + 128] for d in range(4) for p in range(2)]
            out[rnd, j] = tiles_to_rows(jnp.stack(tiles, axis=0).reshape(16, 8, 128)).astype(BF16)

        @pl.loop(1, CTX)
        def _(step):
            j = ring(step)
            turn(j)
            remote(out.at[rnd, j], back_rows(rnd), S_OUT + rnd, R_OUT + rnd, "ctx", j).start()

        turn(me)
        keep = local(out.at[rnd, me], back_rows(rnd), L_OUT + rnd)
        keep.start()
        return keep

    def each_duo(*steps):
        @pl.loop(0, 4, unroll=4)
        def _(d):
            for step in steps:
                step(d)

    def forward_signal(g):
        return lambda d: forward(g, d, spec_s, g)

    def inverse_signal(g):
        return lambda d: inverse(g, d, spec_s, g, 1.0)

    def inverse_grad(g):
        return lambda d: inverse(2 + g, d, spec_g, g, -1.0)

    def forward_grad(g):
        corr[g] = jnp.zeros((256, 256), F32)

        def step(d):
            forward(2 + g, d, spec_g, g)
            for pair in range(2):
                s_re, s_im = spec_s[g, d, pair, :, 0:128], spec_s[g, d, pair, :, 128:256]
                g_re, g_im = spec_g[g, d, pair, :, 0:128], spec_g[g, d, pair, :, 128:256]
                corr[g, :, 0:128] += g_re * s_re + g_im * s_im
                corr[g, :, 128:256] += g_im * s_re - g_re * s_im

        return step

    arrived(0)
    push_all(3)
    each_duo(forward_signal(0), inverse_signal(0))
    kept = [give(0)]
    arrived(2)
    each_duo(forward_grad(0), inverse_grad(0))
    kept.append(give(2))
    arrived(1)
    each_duo(forward_signal(1))
    arrived(3)
    each_duo(forward_grad(1))

    high, low = inverse_mid([corr[0], corr[1]])
    taps = dot(long[512:640, :], high) + dot(long[640:768, :], high) + dot(long[512:640, :], low)
    taps = taps.reshape(CTX, 1, 8, 256)
    taps = jnp.concatenate([taps[..., 0:128], taps[..., 128:256]], axis=1)
    gsend[...] = taps.reshape(CTX, 16, 128).astype(BF16)

    @pl.loop(1, CTX)
    def _(step):
        remote(gsend.at[ring(step)], grecv.at[me], S_FG, R_FG, "ctx", ring(step)).start()

    grecv[me] = gsend[me]
    each_duo(inverse_signal(1))
    kept.append(give(1))

    landed(grecv.at[pl.ds(0, CTX - 1)], R_FG)
    got = grecv[...].astype(F32).reshape(GRL, 8, 128)
    draw[0:GRL, :] = tiles_to_rows(got) * (1.0 / math.sqrt(GSIZE * SEQ)) * env[...]
    draw[GRL:, :] = jnp.zeros((128 - GRL, TOK), F32)
    w3_own = pltpu.roll(w3[...], lax.rem(TP * GRL - tp * GRL, TP * GRL), 1)[:, 0:GRL]
    dact[0:ORDER, :] = dot_full(w3_own, draw[0:GRL, :], ((1,), (0,))) * c2[...]
    dact[ORDER:, :] = dot_full(w2[...], dact[0:ORDER, :], ((1,), (0,))) * c1[...]
    m_feat[...] = dot_full(feat[...], dact[...], ((1,), (1,)))
    g_hid = dot_full(h1a[0:ORDER, :], dact[...], ((1,), (1,)))
    g_out = dot_full(s2[...], draw[...], ((1,), (1,)))
    lane = lax.broadcasted_iota(jnp.int32, (ORDER, 128), 1)
    m_out[...] = jnp.where(lane < ORDER, g_hid, pltpu.roll(g_out, ORDER, 1))
    part[...] = jnp.zeros(part.shape, F32)
    for q in range(CTX):
        part[q, 0:4, :] = m_out[4 * q : 4 * q + 4, :]
        part[q, 4:7, :] = m_feat[3 * q : 3 * q + 3, :]

    @pl.loop(1, CTX)
    def _(step):
        remote(part.at[ring(step)], rs.at[me], S_RS, R_RS, "ctx", ring(step)).start()

    rs[me] = part[me]
    each_duo(inverse_grad(1))
    kept.append(give(3))
    landed(rs.at[pl.ds(0, CTX - 1)], R_RS)
    tpx[tp] = jnp.sum(rs[...], axis=0)

    @pl.loop(1, TP)
    def _(step):
        remote(tpx.at[tp], tpx.at[tp], S_TP, R_TP, "tp", lax.rem(tp + step, TP)).start()

    landed(tpx.at[pl.ds(0, TP - 1)], R_TP)
    agx[me, 0:8, :] = jnp.sum(tpx[...], axis=0)
    row = lax.broadcasted_iota(jnp.int32, (8, 128), 0)
    lane = lax.broadcasted_iota(jnp.int32, (8, 128), 1)
    columns = jnp.zeros((8, 128), F32)
    for k in range(TP):
        piece = pltpu.roll(tpx[k], (GRL * (k % 4) - ORDER) % 128, 1)
        if k >= 4:
            piece = pltpu.roll(piece, 4, 0)
        columns = jnp.where((lane // GRL == k % 4) & (row // 4 == k // 4), piece, columns)
    agx[me, 8:16, :] = columns

    @pl.loop(1, CTX)
    def _(step):
        remote(agx.at[me], agx.at[me], S_AG, R_AG, "ctx", ring(step)).start()

    landed(agx.at[pl.ds(0, CTX - 1)], R_AG)
    final = local(agx, summed, C_SMALL)
    final.start()
    kept.append(final)

    for c in kept:
        c.wait()
    for rnd in range(4):
        landed(back.at[rnd // 2, pl.ds(0, 240), :], R_OUT + rnd)
    for rnd in range(4):
        landed(send.at[rnd, pl.ds(0, CTX - 1)], S_IN + rnd)
        landed(out.at[rnd, pl.ds(0, CTX - 1)], S_OUT + rnd)
    landed(fsend.at[pl.ds(0, CTX - 1)], S_FIL)
    landed(gsend.at[pl.ds(0, CTX - 1)], S_FG)
    landed(part.at[pl.ds(0, CTX - 1)], S_RS)
    landed(tpx.at[pl.ds(0, TP - 1)], S_TP)
    landed(agx.at[pl.ds(0, CTX - 1)], S_AG)


def gate_kernel(
    query, key, value, cot, back, summed, mixed, g_query, g_key, g_value, o_w1, o_b1, o_w2, o_b2, o_w3,
    inner, gates, results, sums, m_feat, sem_in, sem_gate, sem_out, sem_sum,
):
    count = inner.shape[0]
    height = CHL // count
    fetch = [
        [
            pltpu.make_async_copy(back.at[kind, pl.ds(i * height, height), :], inner.at[i, kind], sem_in.at[i, kind])
            for kind in range(2)
        ]
        for i in range(count)
    ]
    given = [
        [
            pltpu.make_async_copy(x.at[pl.ds(i * height, height), :], gates.at[i, k], sem_gate.at[i, k])
            for k, x in enumerate((query, cot, value, key))
        ]
        for i in range(count)
    ]
    for i in range(count):
        for kind in range(2):
            for c in [fetch[i][kind]] + given[i][2 * kind : 2 * kind + 2]:
                c.start()
    load_sums = pltpu.make_async_copy(summed, sums, sem_sum)
    load_sums.start()
    stores = []
    for i in range(count):
        rows = slice(i * height, i * height + height)
        for kind in range(2):
            fetch[i][kind].wait()
            for k in range(2):
                given[i][2 * kind + k].wait()
                results[2 * kind + k, rows, :] = gates[i, 2 * kind + k] * inner[i, kind]
                target = (mixed, g_query, g_key, g_value)[2 * kind + k]
                c = pltpu.make_async_copy(
                    results.at[2 * kind + k, pl.ds(i * height, height), :],
                    target.at[pl.ds(i * height, height), :],
                    sem_out.at[i, 2 * kind + k],
                )
                c.start()
                stores.append(c)
    load_sums.wait()
    for q in range(CTX):
        m_feat[3 * q : 3 * q + 3, :] = sums[q, 4:7, :]
        o_w2[4 * q : 4 * q + 4, :] = sums[q, 0:4, 0:ORDER]
        o_w3[4 * q : 4 * q + 4, 0:128] = sums[q, 8:12, :]
        o_w3[4 * q : 4 * q + 4, 128:256] = sums[q, 12:16, :]
    turned = pltpu.roll(m_feat[...], ORDER, 1)
    o_w1[...] = turned[0:EMB, 0:ORDER]
    o_b1[...] = turned[EMB : EMB + 1, 0:ORDER]
    o_b2[...] = m_feat[EMB : EMB + 1, 0:ORDER]
    for c in stores:
        c.wait()


def on_device(query, key, value, cot, skip, decay, w1, b1, w2, b2, w3):
    wide, thin, long, twid, feat = (jnp.asarray(t) for t in tables())
    f32 = lambda *shape: pltpu.VMEM(shape, F32)
    b16 = lambda *shape: pltpu.VMEM(shape, BF16)
    back, summed = pl.pallas_call(
        mixer_kernel,
        name="mixer",
        out_shape=(
            jax.ShapeDtypeStruct((2, CHL, TOK), BF16),
            jax.ShapeDtypeStruct((CTX, 16, 128), F32),
        ),
        in_specs=[ANY] * 4 + [SMEM] + [ANY] * 11,
        out_specs=(ANY, ANY),
        scratch_shapes=[
            *[b16(CHL, TOK) for _ in range(4)],
            f32(1, GRL), f32(EMB, ORDER), f32(1, ORDER), f32(ORDER, ORDER), f32(1, ORDER), f32(ORDER, TP * GRL),
            b16(*wide.shape), b16(*thin.shape), b16(*long.shape), f32(*twid.shape), f32(64, TOK),
            b16(4, CTX, 4, 16, 256), b16(4, 4, 256, 256),
            f32(2, 4, 2, 256, 256), f32(2, 4, 2, 256, 256), f32(2, 256, 256), f32(2, 256, 256),
            f32(4, 256, 256), b16(4, CTX, 16, TOK),
            f32(FROWS, ORDER), f32(ORDER + 8, ORDER), f32(ORDER + 8, TOK), f32(ORDER, TOK), f32(ORDER, TOK),
            f32(ORDER, TOK), f32(8, GRL), f32(GRL, TOK),
            *[b16(CTX, 16, 128) for _ in range(4)],
            f32(128, TOK), f32(128, TOK), f32(ORDER, 128), f32(ORDER, 128),
            f32(CTX, 8, 128), f32(CTX, 8, 128), f32(TP, 8, 128), f32(CTX, 16, 128),
            pltpu.SemaphoreType.DMA((N_SEM,)),
        ],
        compiler_params=pltpu.CompilerParams(
            collective_id=0, has_side_effects=True, vmem_limit_bytes=56 * 1024 * 1024
        ),
        cost_estimate=pl.CostEstimate(flops=12_000_000_000, bytes_accessed=10_000_000, transcendentals=200_000),
    )(query, key, value, cot, skip, decay[None], w1, b1[None], w2, b2[None], w3, wide, thin, long, twid, feat)
    chunks = 4
    mixed, g_query, g_key, g_value, o_w1, o_b1, o_w2, o_b2, o_w3 = pl.pallas_call(
        gate_kernel,
        name="gates",
        out_shape=tuple(jax.ShapeDtypeStruct((CHL, TOK), BF16) for _ in range(4))
        + tuple(
            jax.ShapeDtypeStruct(s, F32)
            for s in ((EMB, ORDER), (1, ORDER), (ORDER, ORDER), (1, ORDER), (ORDER, TP * GRL))
        ),
        in_specs=[ANY] * 6,
        out_specs=(ANY,) * 4 + (VMEM,) * 5,
        scratch_shapes=[
            b16(chunks, 2, CHL // chunks, TOK), b16(chunks, 4, CHL // chunks, TOK), b16(4, CHL, TOK), f32(CTX, 16, 128), f32(48, 128),
            pltpu.SemaphoreType.DMA((chunks, 2)), pltpu.SemaphoreType.DMA((chunks, 4)), pltpu.SemaphoreType.DMA((chunks, 4)), pltpu.SemaphoreType.DMA,
        ],
        compiler_params=pltpu.CompilerParams(vmem_limit_bytes=63963136),
        cost_estimate=pl.CostEstimate(flops=4_000_000, bytes_accessed=11_000_000, transcendentals=0),
    )(query, key, value, cot, back, summed)
    return mixed, g_query, g_key, g_value, o_w1, o_b1[0], o_w2, o_b2[0], o_w3


def solution(mesh):
    sharded = P("tp", "ctx")
    return jax.shard_map(
        on_device,
        mesh=mesh,
        in_specs=(sharded,) * 4 + (P("tp"), P("tp")) + (P(),) * 5,
        out_specs=(sharded,) * 4 + (P(),) * 5,
        check_vma=False,
    )
```

```python
import functools
import math

import jax
import jax.numpy as jnp
import ml_dtypes
import numpy as np
from jax import lax
from jax.experimental import pallas as pl
from jax.experimental.pallas import tpu as pltpu
from jax.sharding import PartitionSpec as P

MESH = pl.DeviceIdType.MESH
F32 = jnp.float32
BF16 = jnp.bfloat16
HIGHEST = lax.Precision.HIGHEST

SEQ = 16384
FFT = 2 * SEQ
GSIZE = 16
BANDS = 16
EMB = 2 * BANDS + 1
ORDER = 64
CTX = 16
TP = 8
TOK = SEQ // CTX
CHL = 512
GRL = 32
OWN = CHL // CTX
FROWS = 40
ANY = pl.BlockSpec(memory_space=pl.ANY)
VMEM = pl.BlockSpec(memory_space=pltpu.VMEM)
SMEM = pl.BlockSpec(memory_space=pltpu.SMEM)
HBM = pl.BlockSpec(memory_space=pltpu.HBM)

PI_A = 3.140625
PI_B = float(np.float32(math.floor((math.pi - PI_A) * 2.0**22) / 2.0**22))
PI_C = math.pi - PI_A - PI_B


def halves(table):
    high = table.astype(ml_dtypes.bfloat16)
    low = (table - high.astype(np.float64)).astype(ml_dtypes.bfloat16)
    return [high, low]


@functools.cache
def tables():
    k1 = np.arange(256)
    n1 = np.arange(128)
    n2 = np.arange(128)
    outer = 2.0 * np.pi * (np.outer(k1, n1) % 256) / 256.0
    cos1, sin1 = np.cos(outer), np.sin(outer)
    by_rows = lambda first, second: np.stack(
        [first.reshape(256, 16, 8), second.reshape(256, 16, 8)], axis=2
    ).reshape(256, 256)
    fwd = np.concatenate([by_rows(cos1, sin1), by_rows(-sin1, cos1)], axis=0)
    inv = np.concatenate([by_rows(cos1, sin1).T, by_rows(-sin1, cos1).T], axis=1) / FFT
    fwd_real = np.concatenate([cos1, -sin1], axis=0)
    inv_real = np.concatenate([cos1.T, -sin1.T], axis=1) / FFT
    inner = 2.0 * np.pi * (np.outer(n2, n2) % 128) / 128.0
    cos2, sin2 = np.cos(inner), np.sin(inner)
    mid_fwd = np.block([[cos2, -sin2], [sin2, cos2]])
    mid_inv = np.block([[cos2, sin2], [-sin2, cos2]])
    turn = 2.0 * np.pi * np.outer(k1, n2) / FFT
    twiddle = np.concatenate([np.cos(turn), -np.sin(turn)], axis=0).astype(np.float32)
    wide = np.concatenate(halves(fwd) + halves(mid_fwd) + halves(mid_inv), axis=0)
    thin = np.concatenate(halves(fwd_real), axis=0)
    long = np.concatenate(halves(inv) + halves(inv_real), axis=0)
    t = np.arange(SEQ, dtype=np.int64)
    steps = np.array([1 + 3 * SEQ // (8 * 2**b) for b in range(BANDS)], dtype=np.int64)
    phase = 2.0 * np.pi * (np.outer(steps, t) % SEQ) / SEQ
    features = np.zeros((FROWS, SEQ), np.float32)
    features[0] = t / SEQ
    features[1 : 1 + BANDS] = np.cos(phase)
    features[1 + BANDS : EMB] = np.sin(phase)
    features[EMB] = 1.0
    return wide, thin, long, twiddle, features


def dot(left, right):
    return jnp.dot(left, right, preferred_element_type=F32)


def dot_full(left, right, dims):
    return lax.dot_general(
        left, right, (dims, ((), ())), precision=HIGHEST, preferred_element_type=F32
    )


def split(x):
    high = x.astype(BF16)
    return high, (x - high.astype(F32)).astype(BF16)


def sin_cos(x):
    turns = jnp.floor(x * (1.0 / math.pi) + 0.5)
    r = ((x - turns * PI_A) - turns * PI_B) - turns * PI_C
    flip = 1.0 - 2.0 * (turns - 2.0 * jnp.floor(turns * 0.5))
    z = r * r
    sine, cosine = 0.0, 0.0
    for i in range(6, -1, -1):
        sine = sine * z + (-1.0) ** i / math.factorial(2 * i + 1)
        cosine = cosine * z + (-1.0) ** i / math.factorial(2 * i)
    return sine * r * flip, cosine * flip


def rows_to_tiles(x):
    return jnp.transpose(jnp.stack([x[:, 128 * i : 128 * i + 128] for i in range(8)], axis=0), (1, 0, 2))


def tiles_to_rows(x):
    x = jnp.transpose(x, (1, 0, 2))
    return jnp.concatenate([x[i] for i in range(8)], axis=1)


S_IN, R_IN, L_IN = 0, 4, 8
S_OUT, R_OUT, L_OUT = 12, 16, 20
S_FIL, R_FIL, S_FG, R_FG, S_RS, R_RS, S_TP, R_TP, S_AG, R_AG = range(24, 34)
C_ARG, C_TAB, C_SMALL = 34, 38, 43
N_SEM = 49


def mixer_kernel(
    query, key, value, cot, skip, decay_h, w1_h, b1_h, w2_h, b2_h, w3_h, wide_h, thin_h, long_h, twid_h, feat_h,
    back, summed,
    q_v, k_v, v_v, g_v, decay, w1, b1, w2, b2, w3, wide, thin, long, twid, feat,
    send, recv, spec_s, spec_g, spec_f, corr, rows_f, out,
    w1a, w2a, h1a, c1, s2, c2, dec, env, fsend, frecv, gsend, grecv, draw, dact, m_feat, m_out, part, rs, tpx, agx, sem,
):
    me = lax.axis_index("ctx")
    tp = lax.axis_index("tp")

    def ring(step):
        return lax.rem(me + step, CTX)

    barrier = pltpu.get_barrier_semaphore()

    @pl.loop(1, CTX)
    def _(step):
        pl.semaphore_signal(barrier, inc=1, device_id={"ctx": ring(step)}, device_id_type=MESH)

    @pl.loop(1, TP)
    def _(step):
        pl.semaphore_signal(barrier, inc=1, device_id={"tp": lax.rem(tp + step, TP)}, device_id_type=MESH)

    def remote(src, dst, s, r, axis, j):
        return pltpu.make_async_remote_copy(
            src_ref=src, dst_ref=dst, send_sem=sem.at[s], recv_sem=sem.at[r], device_id={axis: j}, device_id_type=MESH
        )

    def local(src, dst, s):
        return pltpu.make_async_copy(src, dst, sem.at[s])

    def landed(ref, s):
        pltpu.make_async_copy(ref, ref, sem.at[s]).wait()

    loads = [local(a, b, C_ARG + i) for i, (a, b) in enumerate(((key, k_v), (value, v_v), (query, q_v), (cot, g_v)))]
    for c in loads:
        c.start()
    rest = [
        local(feat_h.at[:, pl.ds(pl.multiple_of(me * TOK, TOK), TOK)], feat.at[pl.ds(0, FROWS)], C_TAB),
        local(wide_h, wide, C_TAB + 1),
        local(thin_h, thin, C_TAB + 2),
        local(long_h, long, C_TAB + 3),
        local(twid_h, twid, C_TAB + 4),
    ]
    small = [
        local(a, b, C_SMALL + i)
        for i, (a, b) in enumerate(
            ((decay_h, decay), (w1_h, w1), (b1_h, b1), (w2_h, w2), (b2_h, b2), (w3_h, w3))
        )
    ]
    for c in rest[:1] + small + rest[1:]:
        c.start()

    def product(left, right, j, kind):
        rows = pl.ds(pl.multiple_of(j * OWN, OWN), OWN)
        x = left[rows, :].astype(F32) * right[rows, :].astype(F32)
        y = rows_to_tiles(x).reshape(16, 16, 128).astype(BF16)
        for p in range(16):
            send[2 * kind + p // 8, j, p % 8 // 2, :, 128 * (p % 2) : 128 * (p % 2) + 128] = y[p]

    def mine(rnd):
        return recv.at[rnd, :, pl.ds(pl.multiple_of(me * 16, 16), 16), :]

    def push(rnd, j):
        remote(send.at[rnd, j], mine(rnd), S_IN + rnd, R_IN + rnd, "ctx", j).start()

    def push_all(rnd):
        @pl.loop(1, CTX)
        def _(step):
            push(rnd, ring(step))

    loads[0].wait()
    loads[1].wait()
    product(k_v, v_v, me, 0)
    pl.semaphore_wait(barrier, CTX - 1 + TP - 1)

    @pl.loop(1, CTX)
    def _(step):
        product(k_v, v_v, ring(step), 0)
        push(0, ring(step))

    loads[2].wait()
    loads[3].wait()

    @pl.loop(0, CTX)
    def _(j):
        product(q_v, g_v, j, 1)

    push_all(2)
    own = [local(send.at[rnd, me], mine(rnd), L_IN + rnd) for rnd in range(4)]
    for c in own:
        c.start()

    rest[0].wait()
    for c in small:
        c.wait()
    feat[FROWS:, :] = jnp.zeros((64 - FROWS, TOK), F32)
    w1a[...] = jnp.zeros(w1a.shape, F32)
    w1a[0:EMB, :] = w1[...]
    w1a[EMB : EMB + 1, :] = b1[...]
    w2a[...] = jnp.zeros(w2a.shape, F32)
    w2a[0:ORDER, :] = w2[...]
    w2a[ORDER : ORDER + 1, :] = b2[...]
    h1a[ORDER:, :] = (lax.broadcasted_iota(jnp.int32, (8, TOK), 0) == 0).astype(F32)
    sine, cosine = sin_cos(dot_full(w1a[...], feat[0:FROWS, :], ((0,), (0,))))
    h1a[0:ORDER, :] = sine
    c1[...] = cosine
    sine, cosine = sin_cos(dot_full(w2a[...], h1a[...], ((0,), (0,))))
    s2[...] = sine
    c2[...] = cosine
    w3_own = pltpu.roll(w3[...], lax.rem(TP * GRL - tp * GRL, TP * GRL), 1)[:, 0:GRL]
    raw = dot_full(w3_own, s2[...], ((0,), (0,)))
    dec[...] = jnp.zeros(dec.shape, F32)
    dec[0:1, :] = decay[...]
    rate = dot_full(dec[...], h1a[ORDER:, :], ((0,), (0,)))
    position = (me * TOK + lax.broadcasted_iota(jnp.int32, (GRL, TOK), 1)).astype(F32)
    env[...] = jnp.exp(-position * rate) * jnp.sqrt(2.0 * rate + 1.0 / SEQ)
    fsend[...] = rows_to_tiles(raw * env[...]).reshape(CTX, 16, 128).astype(BF16)

    @pl.loop(1, CTX)
    def _(step):
        remote(fsend.at[ring(step)], frecv.at[me], S_FIL, R_FIL, "ctx", ring(step)).start()

    frecv[me] = fsend[me]
    push_all(1)

    for c in rest[1:]:
        c.wait()
    t_re = lambda: twid[0:256, :]
    t_im = lambda: twid[256:512, :]

    def forward_mid(first, pair):
        re = first[0:256, 128 * pair : 128 * pair + 128]
        im = first[256:512, 128 * pair : 128 * pair + 128]
        high, low = split(jnp.concatenate([re * t_re() - im * t_im(), re * t_im() + im * t_re()], axis=1))
        return dot(high, wide[1024:1280, :]) + dot(high, wide[1280:1536, :]) + dot(low, wide[1024:1280, :])

    def inverse_mid(spectra):
        res, ims = [], []
        for spectrum in spectra:
            high, low = split(spectrum)
            x = dot(high, wide[1536:1792, :]) + dot(high, wide[1792:2048, :]) + dot(low, wide[1536:1792, :])
            re, im = x[:, 0:128], x[:, 128:256]
            res.append(re * t_re() + im * t_im())
            ims.append(im * t_re() - re * t_im())
        return split(jnp.concatenate([jnp.concatenate(res, axis=1), jnp.concatenate(ims, axis=1)], axis=0))

    landed(frecv.at[pl.ds(0, CTX - 1)], R_FIL)
    taps = frecv[...].astype(F32).reshape(CTX, 2, 8, 128)
    taps = jnp.concatenate([taps[:, g].reshape(128, 128) for g in range(2)], axis=1).astype(BF16)
    first = dot(thin[0:512, :], taps) + dot(thin[512:1024, :], taps)
    for g in range(2):
        spec_f[g] = forward_mid(first, g)

    def arrived(rnd):
        own[rnd].wait()
        landed(recv.at[rnd, :, pl.ds(0, 240), :], R_IN + rnd)

    def forward(rnd, d, spec, g):
        x = recv[rnd, d]
        first = dot(wide[0:512, :], x) + dot(wide[512:1024, :], x)
        for pair in range(2):
            spec[g, d, pair] = forward_mid(first, pair)

    in_second = lax.broadcasted_iota(jnp.int32, (256, 128), 0) // 8 % 2 == 1

    def inverse(rnd, d, spec, g, sign):
        spectra = []
        for pair in range(2):
            re, im = spec[g, d, pair, :, 0:128], spec[g, d, pair, :, 128:256]
            f_re, f_im = spec_f[g, :, 0:128], sign * spec_f[g, :, 128:256]
            spectra.append(jnp.concatenate([re * f_re - im * f_im, re * f_im + im * f_re], axis=1))
        high, low = inverse_mid(spectra)
        y = dot(long[0:256, :], high) + dot(long[256:512, :], high) + dot(long[0:256, :], low)
        base = me * OWN + g * 16 + d * 4
        scale = jnp.concatenate(
            [jnp.where(in_second, skip[base + 2 * pair + 1], skip[base + 2 * pair]) for pair in range(2)], axis=1
        )
        rows_f[d] = y + scale * recv[rnd, d].astype(F32)

    def back_rows(rnd):
        return back.at[rnd // 2, pl.ds(pl.multiple_of(me * OWN + rnd % 2 * 16, 16), 16), :]

    def give(rnd):
        def turn(j):
            block = pl.ds(pl.multiple_of(j * 16, 16), 16)
            tiles = [rows_f[d, block, 128 * p : 128 * p + 128] for d in range(4) for p in range(2)]
            out[rnd, j] = tiles_to_rows(jnp.stack(tiles, axis=0).reshape(16, 8, 128)).astype(BF16)

        @pl.loop(1, CTX)
        def _(step):
            j = ring(step)
            turn(j)
            remote(out.at[rnd, j], back_rows(rnd), S_OUT + rnd, R_OUT + rnd, "ctx", j).start()

        turn(me)
        keep = local(out.at[rnd, me], back_rows(rnd), L_OUT + rnd)
        keep.start()
        return keep

    def each_duo(*steps):
        @pl.loop(0, 4, unroll=4)
        def _(d):
            for step in steps:
                step(d)

    def forward_signal(g):
        return lambda d: forward(g, d, spec_s, g)

    def inverse_signal(g):
        return lambda d: inverse(g, d, spec_s, g, 1.0)

    def inverse_grad(g):
        return lambda d: inverse(2 + g, d, spec_g, g, -1.0)

    def forward_grad(g):
        corr[g] = jnp.zeros((256, 256), F32)

        def step(d):
            forward(2 + g, d, spec_g, g)
            for pair in range(2):
                s_re, s_im = spec_s[g, d, pair, :, 0:128], spec_s[g, d, pair, :, 128:256]
                g_re, g_im = spec_g[g, d, pair, :, 0:128], spec_g[g, d, pair, :, 128:256]
                corr[g, :, 0:128] += g_re * s_re + g_im * s_im
                corr[g, :, 128:256] += g_im * s_re - g_re * s_im

        return step

    arrived(0)
    push_all(3)
    each_duo(forward_signal(0), inverse_signal(0))
    kept = [give(0)]
    arrived(2)
    each_duo(forward_grad(0), inverse_grad(0))
    kept.append(give(2))
    arrived(1)
    each_duo(forward_signal(1))
    arrived(3)
    each_duo(forward_grad(1))

    high, low = inverse_mid([corr[0], corr[1]])
    taps = dot(long[512:640, :], high) + dot(long[640:768, :], high) + dot(long[512:640, :], low)
    taps = taps.reshape(CTX, 1, 8, 256)
    taps = jnp.concatenate([taps[..., 0:128], taps[..., 128:256]], axis=1)
    gsend[...] = taps.reshape(CTX, 16, 128).astype(BF16)

    @pl.loop(1, CTX)
    def _(step):
        remote(gsend.at[ring(step)], grecv.at[me], S_FG, R_FG, "ctx", ring(step)).start()

    grecv[me] = gsend[me]
    each_duo(inverse_signal(1))
    kept.append(give(1))

    landed(grecv.at[pl.ds(0, CTX - 1)], R_FG)
    got = grecv[...].astype(F32).reshape(GRL, 8, 128)
    draw[0:GRL, :] = tiles_to_rows(got) * (1.0 / math.sqrt(GSIZE * SEQ)) * env[...]
    draw[GRL:, :] = jnp.zeros((128 - GRL, TOK), F32)
    w3_own = pltpu.roll(w3[...], lax.rem(TP * GRL - tp * GRL, TP * GRL), 1)[:, 0:GRL]
    dact[0:ORDER, :] = dot_full(w3_own, draw[0:GRL, :], ((1,), (0,))) * c2[...]
    dact[ORDER:, :] = dot_full(w2[...], dact[0:ORDER, :], ((1,), (0,))) * c1[...]
    m_feat[...] = dot_full(feat[...], dact[...], ((1,), (1,)))
    g_hid = dot_full(h1a[0:ORDER, :], dact[...], ((1,), (1,)))
    g_out = dot_full(s2[...], draw[...], ((1,), (1,)))
    lane = lax.broadcasted_iota(jnp.int32, (ORDER, 128), 1)
    m_out[...] = jnp.where(lane < ORDER, g_hid, pltpu.roll(g_out, ORDER, 1))
    part[...] = jnp.zeros(part.shape, F32)
    for q in range(CTX):
        part[q, 0:4, :] = m_out[4 * q : 4 * q + 4, :]
        part[q, 4:7, :] = m_feat[3 * q : 3 * q + 3, :]

    @pl.loop(1, CTX)
    def _(step):
        remote(part.at[ring(step)], rs.at[me], S_RS, R_RS, "ctx", ring(step)).start()

    rs[me] = part[me]
    each_duo(inverse_grad(1))
    kept.append(give(3))
    landed(rs.at[pl.ds(0, CTX - 1)], R_RS)
    tpx[tp] = jnp.sum(rs[...], axis=0)

    @pl.loop(1, TP)
    def _(step):
        remote(tpx.at[tp], tpx.at[tp], S_TP, R_TP, "tp", lax.rem(tp + step, TP)).start()

    landed(tpx.at[pl.ds(0, TP - 1)], R_TP)
    agx[me, 0:8, :] = jnp.sum(tpx[...], axis=0)
    row = lax.broadcasted_iota(jnp.int32, (8, 128), 0)
    lane = lax.broadcasted_iota(jnp.int32, (8, 128), 1)
    columns = jnp.zeros((8, 128), F32)
    for k in range(TP):
        piece = pltpu.roll(tpx[k], (GRL * (k % 4) - ORDER) % 128, 1)
        if k >= 4:
            piece = pltpu.roll(piece, 4, 0)
        columns = jnp.where((lane // GRL == k % 4) & (row // 4 == k // 4), piece, columns)
    agx[me, 8:16, :] = columns

    @pl.loop(1, CTX)
    def _(step):
        remote(agx.at[me], agx.at[me], S_AG, R_AG, "ctx", ring(step)).start()

    landed(agx.at[pl.ds(0, CTX - 1)], R_AG)
    summed[...] = agx[...]

    for c in kept:
        c.wait()
    for rnd in range(4):
        landed(back.at[rnd // 2, pl.ds(0, 240), :], R_OUT + rnd)
    for rnd in range(4):
        landed(send.at[rnd, pl.ds(0, CTX - 1)], S_IN + rnd)
        landed(out.at[rnd, pl.ds(0, CTX - 1)], S_OUT + rnd)
    landed(fsend.at[pl.ds(0, CTX - 1)], S_FIL)
    landed(gsend.at[pl.ds(0, CTX - 1)], S_FG)
    landed(part.at[pl.ds(0, CTX - 1)], S_RS)
    landed(tpx.at[pl.ds(0, TP - 1)], S_TP)
    landed(agx.at[pl.ds(0, CTX - 1)], S_AG)


def gate_kernel(
    query, key, value, cot, back, summed, mixed, g_query, g_key, g_value, o_w1, o_b1, o_w2, o_b2, o_w3,
    results, m_feat, sem_out,
):
    count = sem_out.shape[0]
    height = CHL // count
    stores = []
    for i in range(count):
        rows = slice(i * height, i * height + height)
        for kind, factors in enumerate(((query, cot), (value, key))):
            for k, factor in enumerate(factors):
                results[2 * kind + k, rows, :] = factor[rows, :] * back[kind, rows, :]
                target = (mixed, g_query, g_key, g_value)[2 * kind + k]
                c = pltpu.make_async_copy(
                    results.at[2 * kind + k, pl.ds(i * height, height), :],
                    target.at[pl.ds(i * height, height), :],
                    sem_out.at[i, 2 * kind + k],
                )
                c.start()
                stores.append(c)
    for q in range(CTX):
        m_feat[3 * q : 3 * q + 3, :] = summed[q, 4:7, :]
        o_w2[4 * q : 4 * q + 4, :] = summed[q, 0:4, 0:ORDER]
        o_w3[4 * q : 4 * q + 4, 0:128] = summed[q, 8:12, :]
        o_w3[4 * q : 4 * q + 4, 128:256] = summed[q, 12:16, :]
    turned = pltpu.roll(m_feat[...], ORDER, 1)
    o_w1[...] = turned[0:EMB, 0:ORDER]
    o_b1[...] = turned[EMB : EMB + 1, 0:ORDER]
    o_b2[...] = m_feat[EMB : EMB + 1, 0:ORDER]
    for c in stores:
        c.wait()


def on_device(query, key, value, cot, skip, decay, w1, b1, w2, b2, w3):
    wide, thin, long, twid, feat = (jnp.asarray(t) for t in tables())
    f32 = lambda *shape: pltpu.VMEM(shape, F32)
    b16 = lambda *shape: pltpu.VMEM(shape, BF16)
    back, summed = pl.pallas_call(
        mixer_kernel,
        name="mixer",
        out_shape=(
            pltpu.VMEM((2, CHL, TOK), BF16),
            pltpu.VMEM((CTX, 16, 128), F32),
        ),
        in_specs=[ANY] * 4 + [SMEM] + [ANY] * 11,
        out_specs=(VMEM, VMEM),
        scratch_shapes=[
            *[b16(CHL, TOK) for _ in range(4)],
            f32(1, GRL), f32(EMB, ORDER), f32(1, ORDER), f32(ORDER, ORDER), f32(1, ORDER), f32(ORDER, TP * GRL),
            b16(*wide.shape), b16(*thin.shape), b16(*long.shape), f32(*twid.shape), f32(64, TOK),
            b16(4, CTX, 4, 16, 256), b16(4, 4, 256, 256),
            f32(2, 4, 2, 256, 256), f32(2, 4, 2, 256, 256), f32(2, 256, 256), f32(2, 256, 256),
            f32(4, 256, 256), b16(4, CTX, 16, TOK),
            f32(FROWS, ORDER), f32(ORDER + 8, ORDER), f32(ORDER + 8, TOK), f32(ORDER, TOK), f32(ORDER, TOK),
            f32(ORDER, TOK), f32(8, GRL), f32(GRL, TOK),
            *[b16(CTX, 16, 128) for _ in range(4)],
            f32(128, TOK), f32(128, TOK), f32(ORDER, 128), f32(ORDER, 128),
            f32(CTX, 8, 128), f32(CTX, 8, 128), f32(TP, 8, 128), f32(CTX, 16, 128),
            pltpu.SemaphoreType.DMA((N_SEM,)),
        ],
        compiler_params=pltpu.CompilerParams(
            collective_id=0, has_side_effects=True, vmem_limit_bytes=56 * 1024 * 1024
        ),
        cost_estimate=pl.CostEstimate(flops=12_000_000_000, bytes_accessed=10_000_000, transcendentals=200_000),
    )(query, key, value, cot, skip, decay[None], w1, b1[None], w2, b2[None], w3, wide, thin, long, twid, feat)
    chunks = 4
    mixed, g_query, g_key, g_value, o_w1, o_b1, o_w2, o_b2, o_w3 = pl.pallas_call(
        gate_kernel,
        name="gates",
        out_shape=tuple(jax.ShapeDtypeStruct((CHL, TOK), BF16) for _ in range(4))
        + tuple(
            jax.ShapeDtypeStruct(s, F32)
            for s in ((EMB, ORDER), (1, ORDER), (ORDER, ORDER), (1, ORDER), (ORDER, TP * GRL))
        ),
        in_specs=[VMEM] * 6,
        out_specs=(ANY,) * 4 + (VMEM,) * 5,
        scratch_shapes=[
            b16(4, CHL, TOK), f32(48, 128), pltpu.SemaphoreType.DMA((chunks, 4)),
        ],
        compiler_params=pltpu.CompilerParams(vmem_limit_bytes=32 * 1024 * 1024),
        cost_estimate=pl.CostEstimate(flops=4_000_000, bytes_accessed=11_000_000, transcendentals=0),
    )(query, key, value, cot, back, summed)
    return mixed, g_query, g_key, g_value, o_w1, o_b1[0], o_w2, o_b2[0], o_w3


def solution(mesh):
    sharded = P("tp", "ctx")
    return jax.shard_map(
        on_device,
        mesh=mesh,
        in_specs=(sharded,) * 4 + (P("tp"), P("tp")) + (P(),) * 5,
        out_specs=(sharded,) * 4 + (P(),) * 5,
        check_vma=False,
    )
```

```python
import functools
import math

import jax
import jax.numpy as jnp
import ml_dtypes
import numpy as np
from jax import lax
from jax.experimental import pallas as pl
from jax.experimental.pallas import tpu as pltpu
from jax.sharding import PartitionSpec as P

MESH = pl.DeviceIdType.MESH
F32 = jnp.float32
BF16 = jnp.bfloat16
HIGHEST = lax.Precision.HIGHEST

SEQ = 16384
FFT = 2 * SEQ
GSIZE = 16
BANDS = 16
EMB = 2 * BANDS + 1
ORDER = 64
CTX = 16
TP = 8
TOK = SEQ // CTX
CHL = 512
GRL = 32
OWN = CHL // CTX
FROWS = 40
ANY = pl.BlockSpec(memory_space=pl.ANY)
VMEM = pl.BlockSpec(memory_space=pltpu.VMEM)
SMEM = pl.BlockSpec(memory_space=pltpu.SMEM)
HBM = pl.BlockSpec(memory_space=pltpu.HBM)

PI_A = 3.140625
PI_B = float(np.float32(math.floor((math.pi - PI_A) * 2.0**22) / 2.0**22))
PI_C = math.pi - PI_A - PI_B


def halves(table):
    high = table.astype(ml_dtypes.bfloat16)
    low = (table - high.astype(np.float64)).astype(ml_dtypes.bfloat16)
    return [high, low]


@functools.cache
def tables():
    k1 = np.arange(256)
    n1 = np.arange(128)
    n2 = np.arange(128)
    outer = 2.0 * np.pi * (np.outer(k1, n1) % 256) / 256.0
    cos1, sin1 = np.cos(outer), np.sin(outer)
    by_rows = lambda first, second: np.stack(
        [first.reshape(256, 16, 8), second.reshape(256, 16, 8)], axis=2
    ).reshape(256, 256)
    fwd = np.concatenate([by_rows(cos1, sin1), by_rows(-sin1, cos1)], axis=0)
    inv = np.concatenate([by_rows(cos1, sin1).T, by_rows(-sin1, cos1).T], axis=1) / FFT
    fwd_real = np.concatenate([cos1, -sin1], axis=0)
    inv_real = np.concatenate([cos1.T, -sin1.T], axis=1) / FFT
    inner = 2.0 * np.pi * (np.outer(n2, n2) % 128) / 128.0
    cos2, sin2 = np.cos(inner), np.sin(inner)
    mid_fwd = np.block([[cos2, -sin2], [sin2, cos2]])
    mid_inv = np.block([[cos2, sin2], [-sin2, cos2]])
    turn = 2.0 * np.pi * np.outer(k1, n2) / FFT
    twiddle = np.concatenate([np.cos(turn), -np.sin(turn)], axis=0).astype(np.float32)
    wide = np.concatenate(halves(fwd) + halves(mid_fwd) + halves(mid_inv), axis=0)
    thin = np.concatenate(halves(fwd_real), axis=0)
    long = np.concatenate(halves(inv) + halves(inv_real), axis=0)
    t = np.arange(SEQ, dtype=np.int64)
    steps = np.array([1 + 3 * SEQ // (8 * 2**b) for b in range(BANDS)], dtype=np.int64)
    phase = 2.0 * np.pi * (np.outer(steps, t) % SEQ) / SEQ
    features = np.zeros((FROWS, SEQ), np.float32)
    features[0] = t / SEQ
    features[1 : 1 + BANDS] = np.cos(phase)
    features[1 + BANDS : EMB] = np.sin(phase)
    features[EMB] = 1.0
    return wide, thin, long, twiddle, features


def dot(left, right):
    return jnp.dot(left, right, preferred_element_type=F32)


def dot_full(left, right, dims):
    return lax.dot_general(
        left, right, (dims, ((), ())), precision=HIGHEST, preferred_element_type=F32
    )


def dot_three(left, right, dims):
    return lax.dot_general(
        left, right, (dims, ((), ())), precision=lax.Precision.HIGH, preferred_element_type=F32
    )


def split(x):
    high = x.astype(BF16)
    return high, (x - high.astype(F32)).astype(BF16)


def sin_cos(x):
    turns = jnp.floor(x * (1.0 / math.pi) + 0.5)
    r = ((x - turns * PI_A) - turns * PI_B) - turns * PI_C
    flip = 1.0 - 2.0 * (turns - 2.0 * jnp.floor(turns * 0.5))
    z = r * r
    sine, cosine = 0.0, 0.0
    for i in range(6, -1, -1):
        sine = sine * z + (-1.0) ** i / math.factorial(2 * i + 1)
        cosine = cosine * z + (-1.0) ** i / math.factorial(2 * i)
    return sine * r * flip, cosine * flip


def rows_to_tiles(x):
    return jnp.transpose(jnp.stack([x[:, 128 * i : 128 * i + 128] for i in range(8)], axis=0), (1, 0, 2))


def tiles_to_rows(x):
    x = jnp.transpose(x, (1, 0, 2))
    return jnp.concatenate([x[i] for i in range(8)], axis=1)


S_IN, R_IN, L_IN = 0, 4, 8
S_OUT, R_OUT, L_OUT = 12, 16, 20
S_FIL, R_FIL, S_FG, R_FG, S_RS, R_RS, S_CX, R_CX, S_AG, R_AG = range(24, 34)
C_ARG, C_TAB, C_SMALL = 34, 38, 43
N_SEM = 49


def mixer_kernel(
    query, key, value, cot, skip, decay_h, w1_h, b1_h, w2_h, b2_h, w3_h, wide_h, thin_h, long_h, twid_h, feat_h,
    back, summed,
    q_v, k_v, v_v, g_v, decay, w1, b1, w2, b2, w3, wide, thin, long, twid, feat,
    send, recv, spec_s, spec_g, spec_f, corr, rows_f, out,
    w1a, w2a, h1a, c1, s2, c2, dec, env, fsend, frecv, gsend, grecv, draw, dact, m_feat, part, eighths, cx, agx, sem,
):
    me = lax.axis_index("ctx")
    tp = lax.axis_index("tp")

    def ring(step):
        return lax.rem(me + step, CTX)

    barrier = pltpu.get_barrier_semaphore()

    @pl.loop(1, CTX)
    def _(step):
        pl.semaphore_signal(barrier, inc=1, device_id={"ctx": ring(step)}, device_id_type=MESH)

    @pl.loop(1, TP)
    def _(step):
        pl.semaphore_signal(barrier, inc=1, device_id={"tp": lax.rem(tp + step, TP)}, device_id_type=MESH)

    def remote(src, dst, s, r, axis, j):
        return pltpu.make_async_remote_copy(
            src_ref=src, dst_ref=dst, send_sem=sem.at[s], recv_sem=sem.at[r], device_id={axis: j}, device_id_type=MESH
        )

    def local(src, dst, s):
        return pltpu.make_async_copy(src, dst, sem.at[s])

    def landed(ref, s):
        pltpu.make_async_copy(ref, ref, sem.at[s]).wait()

    loads = [local(a, b, C_ARG + i) for i, (a, b) in enumerate(((key, k_v), (value, v_v), (query, q_v), (cot, g_v)))]
    for c in loads:
        c.start()
    rest = [
        local(feat_h.at[:, pl.ds(pl.multiple_of(me * TOK, TOK), TOK)], feat.at[pl.ds(0, FROWS)], C_TAB),
        local(wide_h, wide, C_TAB + 1),
        local(thin_h, thin, C_TAB + 2),
        local(long_h, long, C_TAB + 3),
        local(twid_h, twid, C_TAB + 4),
    ]
    small = [
        local(a, b, C_SMALL + i)
        for i, (a, b) in enumerate(
            ((decay_h, decay), (w1_h, w1), (b1_h, b1), (w2_h, w2), (b2_h, b2), (w3_h, w3))
        )
    ]
    for c in rest[:1] + small + rest[1:]:
        c.start()

    def product(left, right, j, kind):
        rows = pl.ds(pl.multiple_of(j * OWN, OWN), OWN)
        x = left[rows, :].astype(F32) * right[rows, :].astype(F32)
        y = rows_to_tiles(x).reshape(16, 16, 128).astype(BF16)
        for p in range(16):
            send[2 * kind + p // 8, j, p % 8 // 2, :, 128 * (p % 2) : 128 * (p % 2) + 128] = y[p]

    def mine(rnd):
        return recv.at[rnd, :, pl.ds(pl.multiple_of(me * 16, 16), 16), :]

    def push(rnd, j):
        remote(send.at[rnd, j], mine(rnd), S_IN + rnd, R_IN + rnd, "ctx", j).start()

    def push_all(rnd):
        @pl.loop(1, CTX)
        def _(step):
            push(rnd, ring(step))

    loads[0].wait()
    loads[1].wait()
    product(k_v, v_v, me, 0)
    pl.semaphore_wait(barrier, CTX - 1 + TP - 1)

    @pl.loop(1, CTX)
    def _(step):
        product(k_v, v_v, ring(step), 0)
        push(0, ring(step))

    loads[2].wait()
    loads[3].wait()

    @pl.loop(0, CTX)
    def _(j):
        product(q_v, g_v, j, 1)

    push_all(2)
    own = [local(send.at[rnd, me], mine(rnd), L_IN + rnd) for rnd in range(4)]
    for c in own:
        c.start()

    rest[0].wait()
    for c in small:
        c.wait()
    feat[FROWS:, :] = jnp.zeros((64 - FROWS, TOK), F32)
    w1a[...] = jnp.zeros(w1a.shape, F32)
    w1a[0:EMB, :] = w1[...]
    w1a[EMB : EMB + 1, :] = b1[...]
    w2a[...] = jnp.zeros(w2a.shape, F32)
    w2a[0:ORDER, :] = w2[...]
    w2a[ORDER : ORDER + 1, :] = b2[...]
    h1a[ORDER:, :] = (lax.broadcasted_iota(jnp.int32, (8, TOK), 0) == 0).astype(F32)
    sine, cosine = sin_cos(dot_full(w1a[...], feat[0:FROWS, :], ((0,), (0,))))
    h1a[0:ORDER, :] = sine
    c1[...] = cosine
    sine, cosine = sin_cos(dot_full(w2a[...], h1a[...], ((0,), (0,))))
    s2[...] = sine
    c2[...] = cosine
    w3_own = pltpu.roll(w3[...], lax.rem(TP * GRL - tp * GRL, TP * GRL), 1)[:, 0:GRL]
    raw = dot_full(w3_own, s2[...], ((0,), (0,)))
    dec[...] = jnp.zeros(dec.shape, F32)
    dec[0:1, :] = decay[...]
    rate = dot_full(dec[...], h1a[ORDER:, :], ((0,), (0,)))
    position = (me * TOK + lax.broadcasted_iota(jnp.int32, (GRL, TOK), 1)).astype(F32)
    env[...] = jnp.exp(-position * rate) * jnp.sqrt(2.0 * rate + 1.0 / SEQ)
    fsend[...] = rows_to_tiles(raw * env[...]).reshape(CTX, 16, 128).astype(BF16)

    @pl.loop(1, CTX)
    def _(step):
        remote(fsend.at[ring(step)], frecv.at[me], S_FIL, R_FIL, "ctx", ring(step)).start()

    frecv[me] = fsend[me]
    push_all(1)

    for c in rest[1:]:
        c.wait()
    t_re = lambda: twid[0:256, :]
    t_im = lambda: twid[256:512, :]

    def forward_mid(first, pair):
        re = first[0:256, 128 * pair : 128 * pair + 128]
        im = first[256:512, 128 * pair : 128 * pair + 128]
        high, low = split(jnp.concatenate([re * t_re() - im * t_im(), re * t_im() + im * t_re()], axis=1))
        return dot(high, wide[1024:1280, :]) + dot(high, wide[1280:1536, :]) + dot(low, wide[1024:1280, :])

    def inverse_mid(spectra):
        res, ims = [], []
        for spectrum in spectra:
            high, low = split(spectrum)
            x = dot(high, wide[1536:1792, :]) + dot(high, wide[1792:2048, :]) + dot(low, wide[1536:1792, :])
            re, im = x[:, 0:128], x[:, 128:256]
            res.append(re * t_re() + im * t_im())
            ims.append(im * t_re() - re * t_im())
        return split(jnp.concatenate([jnp.concatenate(res, axis=1), jnp.concatenate(ims, axis=1)], axis=0))

    landed(frecv.at[pl.ds(0, CTX - 1)], R_FIL)
    taps = frecv[...].astype(F32).reshape(CTX, 2, 8, 128)
    taps = jnp.concatenate([taps[:, g].reshape(128, 128) for g in range(2)], axis=1).astype(BF16)
    first = dot(thin[0:512, :], taps) + dot(thin[512:1024, :], taps)
    for g in range(2):
        spec_f[g] = forward_mid(first, g)

    def arrived(rnd):
        own[rnd].wait()
        landed(recv.at[rnd, :, pl.ds(0, 240), :], R_IN + rnd)

    def forward(rnd, d, spec, g):
        x = recv[rnd, d]
        first = dot(wide[0:512, :], x) + dot(wide[512:1024, :], x)
        for pair in range(2):
            spec[g, d, pair] = forward_mid(first, pair)

    in_second = lax.broadcasted_iota(jnp.int32, (256, 128), 0) // 8 % 2 == 1

    def inverse(rnd, d, spec, g, sign):
        spectra = []
        for pair in range(2):
            re, im = spec[g, d, pair, :, 0:128], spec[g, d, pair, :, 128:256]
            f_re, f_im = spec_f[g, :, 0:128], sign * spec_f[g, :, 128:256]
            spectra.append(jnp.concatenate([re * f_re - im * f_im, re * f_im + im * f_re], axis=1))
        high, low = inverse_mid(spectra)
        y = dot(long[0:256, :], high) + dot(long[256:512, :], high) + dot(long[0:256, :], low)
        base = me * OWN + g * 16 + d * 4
        scale = jnp.concatenate(
            [jnp.where(in_second, skip[base + 2 * pair + 1], skip[base + 2 * pair]) for pair in range(2)], axis=1
        )
        rows_f[d] = y + scale * recv[rnd, d].astype(F32)

    def back_rows(rnd):
        return back.at[rnd // 2, pl.ds(pl.multiple_of(me * OWN + rnd % 2 * 16, 16), 16), :]

    def turn_all(rnd):
        @pl.loop(0, CTX)
        def _(j):
            block = pl.ds(pl.multiple_of(j * 16, 16), 16)
            tiles = [rows_f[d, block, 128 * p : 128 * p + 128] for d in range(4) for p in range(2)]
            out[rnd, j] = tiles_to_rows(jnp.stack(tiles, axis=0).reshape(16, 8, 128)).astype(BF16)

    kept = []

    def send_out(rnd):
        @pl.loop(1, CTX)
        def _(step):
            j = ring(step)
            remote(out.at[rnd, j], back_rows(rnd), S_OUT + rnd, R_OUT + rnd, "ctx", j).start()

        keep = local(out.at[rnd, me], back_rows(rnd), L_OUT + rnd)
        keep.start()
        kept.append(keep)

    def each_duo(*steps):
        @pl.loop(0, 4, unroll=4)
        def _(d):
            for step in steps:
                step(d)

    def forward_signal(g):
        return lambda d: forward(g, d, spec_s, g)

    def inverse_signal(g):
        return lambda d: inverse(g, d, spec_s, g, 1.0)

    def inverse_grad(g):
        return lambda d: inverse(2 + g, d, spec_g, g, -1.0)

    def forward_grad(g):
        corr[g] = jnp.zeros((256, 256), F32)

        def step(d):
            forward(2 + g, d, spec_g, g)
            for pair in range(2):
                s_re, s_im = spec_s[g, d, pair, :, 0:128], spec_s[g, d, pair, :, 128:256]
                g_re, g_im = spec_g[g, d, pair, :, 0:128], spec_g[g, d, pair, :, 128:256]
                corr[g, :, 0:128] += g_re * s_re + g_im * s_im
                corr[g, :, 128:256] += g_im * s_re - g_re * s_im

        return step

    arrived(0)
    push_all(3)
    each_duo(forward_signal(0), inverse_signal(0))
    turn_all(0)
    send_out(0)
    arrived(2)
    each_duo(forward_grad(0), inverse_grad(0))
    turn_all(2)
    send_out(2)
    arrived(1)
    each_duo(forward_signal(1))
    arrived(3)
    each_duo(forward_grad(1))

    high, low = inverse_mid([corr[0], corr[1]])
    taps = dot(long[512:640, :], high) + dot(long[640:768, :], high) + dot(long[512:640, :], low)
    taps = taps.reshape(CTX, 1, 8, 256)
    taps = jnp.concatenate([taps[..., 0:128], taps[..., 128:256]], axis=1)
    gsend[...] = taps.reshape(CTX, 16, 128).astype(BF16)

    @pl.loop(1, CTX)
    def _(step):
        remote(gsend.at[ring(step)], grecv.at[me], S_FG, R_FG, "ctx", ring(step)).start()

    grecv[me] = gsend[me]
    each_duo(inverse_signal(1))
    turn_all(1)

    landed(grecv.at[pl.ds(0, CTX - 1)], R_FG)
    got = grecv[...].astype(F32).reshape(GRL, 8, 128)
    draw[0:GRL, :] = tiles_to_rows(got) * (1.0 / math.sqrt(GSIZE * SEQ)) * env[...]
    draw[GRL:, :] = jnp.zeros((128 - GRL, TOK), F32)
    w3_own = pltpu.roll(w3[...], lax.rem(TP * GRL - tp * GRL, TP * GRL), 1)[:, 0:GRL]
    dact[0:ORDER, :] = dot_three(w3_own, draw[0:GRL, :], ((1,), (0,))) * c2[...]
    dact[ORDER:, :] = dot_three(w2[...], dact[0:ORDER, :], ((1,), (0,))) * c1[...]
    m_feat[...] = dot_three(feat[...], dact[...], ((1,), (1,)))
    m_feat[EMB + 1 : EMB + 2, :] = pltpu.roll(m_feat[...], ORDER, 1)[EMB : EMB + 1, :]
    g_hid = dot_three(h1a[0:ORDER, :], dact[...], ((1,), (1,)))
    g_out = dot_three(s2[...], draw[...], ((1,), (1,)))
    lane = lax.broadcasted_iota(jnp.int32, (8, 128), 1)
    for k in range(TP):
        part[k] = jnp.where(lane < ORDER, g_hid[8 * k : 8 * k + 8, :], m_feat[5 * k : 5 * k + 8, :])
    cx[me, 8:24, :] = sum(pltpu.roll(g_out[16 * i : 16 * i + 16, :], GRL * i, 1) for i in range(4))

    @pl.loop(1, TP)
    def _(step):
        k = lax.rem(tp + step, TP)
        remote(part.at[k], eighths.at[tp], S_RS, R_RS, "tp", k).start()

    eighths[tp] = part[tp]
    send_out(1)
    each_duo(inverse_grad(1))
    turn_all(3)
    landed(eighths.at[pl.ds(0, TP - 1)], R_RS)
    cx[me, 0:8, :] = jnp.sum(eighths[...], axis=0)

    @pl.loop(1, CTX)
    def _(step):
        remote(cx.at[me], cx.at[me], S_CX, R_CX, "ctx", ring(step)).start()

    send_out(3)
    landed(cx.at[pl.ds(0, CTX - 1)], R_CX)
    agx[tp] = jnp.sum(cx[...], axis=0)

    @pl.loop(1, TP)
    def _(step):
        remote(agx.at[tp], agx.at[tp], S_AG, R_AG, "tp", lax.rem(tp + step, TP)).start()

    landed(agx.at[pl.ds(0, TP - 1)], R_AG)
    summed[...] = agx[...]

    for c in kept:
        c.wait()
    for rnd in range(4):
        landed(back.at[rnd // 2, pl.ds(0, 240), :], R_OUT + rnd)
    for rnd in range(4):
        landed(send.at[rnd, pl.ds(0, CTX - 1)], S_IN + rnd)
        landed(out.at[rnd, pl.ds(0, CTX - 1)], S_OUT + rnd)
    landed(fsend.at[pl.ds(0, CTX - 1)], S_FIL)
    landed(gsend.at[pl.ds(0, CTX - 1)], S_FG)
    landed(part.at[pl.ds(0, TP - 1)], S_RS)
    landed(cx.at[pl.ds(0, CTX - 1)], S_CX)
    landed(agx.at[pl.ds(0, TP - 1)], S_AG)


def gate_kernel(
    query, key, value, cot, back, summed, mixed, g_query, g_key, g_value, o_w1, o_b1, o_w2, o_b2, o_w3,
    results, m_feat, sem_out,
):
    count = sem_out.shape[0]
    height = CHL // count
    stores = []
    for i in range(count):
        rows = slice(i * height, i * height + height)
        for kind, factors in enumerate(((query, cot), (value, key))):
            for k, factor in enumerate(factors):
                results[2 * kind + k, rows, :] = factor[rows, :] * back[kind, rows, :]
                target = (mixed, g_query, g_key, g_value)[2 * kind + k]
                c = pltpu.make_async_copy(
                    results.at[2 * kind + k, pl.ds(i * height, height), :],
                    target.at[pl.ds(i * height, height), :],
                    sem_out.at[i, 2 * kind + k],
                )
                c.start()
                stores.append(c)
    for k in range(TP):
        m_feat[5 * k : 5 * k + 5, :] = summed[k, 0:5, :]
        o_w2[8 * k : 8 * k + 8, :] = summed[k, 0:8, 0:ORDER]
    lane = lax.broadcasted_iota(jnp.int32, (16, 128), 1) // GRL
    for half in range(2):
        for i in range(4):
            block = jnp.zeros((16, 128), F32)
            for k in range(4):
                turned = pltpu.roll(summed[4 * half + k, 8:24, :], GRL * (k - i) % 128, 1)
                block = jnp.where(lane == k, turned, block)
            o_w3[16 * i : 16 * i + 16, 128 * half : 128 * half + 128] = block
    feat = pltpu.roll(m_feat[...], ORDER, 1)
    o_w1[...] = feat[0:EMB, 0:ORDER]
    o_b1[...] = feat[EMB : EMB + 1, 0:ORDER]
    o_b2[...] = feat[EMB + 1 : EMB + 2, 0:ORDER]
    for c in stores:
        c.wait()


def on_device(query, key, value, cot, skip, decay, w1, b1, w2, b2, w3):
    wide, thin, long, twid, feat = (jnp.asarray(t) for t in tables())
    f32 = lambda *shape: pltpu.VMEM(shape, F32)
    b16 = lambda *shape: pltpu.VMEM(shape, BF16)
    back, summed = pl.pallas_call(
        mixer_kernel,
        name="mixer",
        out_shape=(
            pltpu.VMEM((2, CHL, TOK), BF16),
            pltpu.VMEM((TP, 24, 128), F32),
        ),
        in_specs=[ANY] * 4 + [SMEM] + [ANY] * 11,
        out_specs=(VMEM, VMEM),
        scratch_shapes=[
            *[b16(CHL, TOK) for _ in range(4)],
            f32(1, GRL), f32(EMB, ORDER), f32(1, ORDER), f32(ORDER, ORDER), f32(1, ORDER), f32(ORDER, TP * GRL),
            b16(*wide.shape), b16(*thin.shape), b16(*long.shape), f32(*twid.shape), f32(64, TOK),
            b16(4, CTX, 4, 16, 256), b16(4, 4, 256, 256),
            f32(2, 4, 2, 256, 256), f32(2, 4, 2, 256, 256), f32(2, 256, 256), f32(2, 256, 256),
            f32(4, 256, 256), b16(4, CTX, 16, TOK),
            f32(FROWS, ORDER), f32(ORDER + 8, ORDER), f32(ORDER + 8, TOK), f32(ORDER, TOK), f32(ORDER, TOK),
            f32(ORDER, TOK), f32(8, GRL), f32(GRL, TOK),
            *[b16(CTX, 16, 128) for _ in range(4)],
            f32(128, TOK), f32(128, TOK), f32(ORDER, 128),
            f32(TP, 8, 128), f32(TP, 8, 128), f32(CTX, 24, 128), f32(TP, 24, 128),
            pltpu.SemaphoreType.DMA((N_SEM,)),
        ],
        compiler_params=pltpu.CompilerParams(
            collective_id=0, has_side_effects=True, vmem_limit_bytes=56 * 1024 * 1024
        ),
        cost_estimate=pl.CostEstimate(flops=12_000_000_000, bytes_accessed=10_000_000, transcendentals=200_000),
    )(query, key, value, cot, skip, decay[None], w1, b1[None], w2, b2[None], w3, wide, thin, long, twid, feat)
    chunks = 4
    mixed, g_query, g_key, g_value, o_w1, o_b1, o_w2, o_b2, o_w3 = pl.pallas_call(
        gate_kernel,
        name="gates",
        out_shape=tuple(jax.ShapeDtypeStruct((CHL, TOK), BF16) for _ in range(4))
        + tuple(
            jax.ShapeDtypeStruct(s, F32)
            for s in ((EMB, ORDER), (1, ORDER), (ORDER, ORDER), (1, ORDER), (ORDER, TP * GRL))
        ),
        in_specs=[VMEM] * 6,
        out_specs=(ANY,) * 4 + (VMEM,) * 5,
        scratch_shapes=[
            b16(4, CHL, TOK), f32(FROWS, 128), pltpu.SemaphoreType.DMA((chunks, 4)),
        ],
        compiler_params=pltpu.CompilerParams(vmem_limit_bytes=32 * 1024 * 1024),
        cost_estimate=pl.CostEstimate(flops=4_000_000, bytes_accessed=11_000_000, transcendentals=0),
    )(query, key, value, cot, back, summed)
    return mixed, g_query, g_key, g_value, o_w1, o_b1[0], o_w2, o_b2[0], o_w3


def solution(mesh):
    sharded = P("tp", "ctx")
    return jax.shard_map(
        on_device,
        mesh=mesh,
        in_specs=(sharded,) * 4 + (P("tp"), P("tp")) + (P(),) * 5,
        out_specs=(sharded,) * 4 + (P(),) * 5,
        check_vma=False,
    )
```

```python
import functools
import math

import jax
import jax.numpy as jnp
import ml_dtypes
import numpy as np
from jax import lax
from jax.experimental import pallas as pl
from jax.experimental.pallas import tpu as pltpu
from jax.sharding import PartitionSpec as P

MESH = pl.DeviceIdType.MESH
F32 = jnp.float32
BF16 = jnp.bfloat16
HIGHEST = lax.Precision.HIGHEST

SEQ = 16384
FFT = 2 * SEQ
GSIZE = 16
BANDS = 16
EMB = 2 * BANDS + 1
ORDER = 64
CTX = 16
TP = 8
TOK = SEQ // CTX
CHL = 512
GRL = 32
OWN = CHL // CTX
FROWS = 40
ANY = pl.BlockSpec(memory_space=pl.ANY)
VMEM = pl.BlockSpec(memory_space=pltpu.VMEM)
SMEM = pl.BlockSpec(memory_space=pltpu.SMEM)
HBM = pl.BlockSpec(memory_space=pltpu.HBM)

PI_A = 3.140625
PI_B = float(np.float32(math.floor((math.pi - PI_A) * 2.0**22) / 2.0**22))
PI_C = math.pi - PI_A - PI_B


def halves(table):
    high = table.astype(ml_dtypes.bfloat16)
    low = (table - high.astype(np.float64)).astype(ml_dtypes.bfloat16)
    return [high, low]


@functools.cache
def tables():
    k1 = np.arange(256)
    n1 = np.arange(128)
    n2 = np.arange(128)
    outer = 2.0 * np.pi * (np.outer(k1, n1) % 256) / 256.0
    cos1, sin1 = np.cos(outer), np.sin(outer)
    by_rows = lambda first, second: np.stack(
        [first.reshape(256, 16, 8), second.reshape(256, 16, 8)], axis=2
    ).reshape(256, 256)
    fwd = np.concatenate([by_rows(cos1, sin1), by_rows(-sin1, cos1)], axis=0)
    inv = np.concatenate([by_rows(cos1, sin1).T, by_rows(-sin1, cos1).T], axis=1) / FFT
    fwd_real = np.concatenate([cos1, -sin1], axis=0)
    inv_real = np.concatenate([cos1.T, -sin1.T], axis=1) / FFT
    inner = 2.0 * np.pi * (np.outer(n2, n2) % 128) / 128.0
    cos2, sin2 = np.cos(inner), np.sin(inner)
    mid_fwd = np.block([[cos2, -sin2], [sin2, cos2]])
    mid_inv = np.block([[cos2, sin2], [-sin2, cos2]])
    turn = 2.0 * np.pi * np.outer(k1, n2) / FFT
    twiddle = np.concatenate([np.cos(turn), -np.sin(turn)], axis=0).astype(np.float32)
    wide = np.concatenate(halves(fwd) + halves(mid_fwd) + halves(mid_inv), axis=0)
    thin = np.concatenate(halves(fwd_real), axis=0)
    long = np.concatenate(halves(inv) + halves(inv_real), axis=0)
    t = np.arange(SEQ, dtype=np.int64)
    steps = np.array([1 + 3 * SEQ // (8 * 2**b) for b in range(BANDS)], dtype=np.int64)
    phase = 2.0 * np.pi * (np.outer(steps, t) % SEQ) / SEQ
    features = np.zeros((FROWS, SEQ), np.float32)
    features[0] = t / SEQ
    features[1 : 1 + BANDS] = np.cos(phase)
    features[1 + BANDS : EMB] = np.sin(phase)
    features[EMB] = 1.0
    return wide, thin, long, twiddle, features


def dot(left, right):
    return jnp.dot(left, right, preferred_element_type=F32)


def dot_full(left, right, dims):
    return lax.dot_general(
        left, right, (dims, ((), ())), precision=HIGHEST, preferred_element_type=F32
    )


def dot_three(left, right, dims):
    return lax.dot_general(
        left, right, (dims, ((), ())), precision=lax.Precision.HIGH, preferred_element_type=F32
    )


def split(x):
    high = x.astype(BF16)
    return high, (x - high.astype(F32)).astype(BF16)


def sin_cos(x):
    turns = jnp.floor(x * (1.0 / math.pi) + 0.5)
    r = ((x - turns * PI_A) - turns * PI_B) - turns * PI_C
    flip = 1.0 - 2.0 * (turns - 2.0 * jnp.floor(turns * 0.5))
    z = r * r
    sine, cosine = 0.0, 0.0
    for i in range(6, -1, -1):
        sine = sine * z + (-1.0) ** i / math.factorial(2 * i + 1)
        cosine = cosine * z + (-1.0) ** i / math.factorial(2 * i)
    return sine * r * flip, cosine * flip


def rows_to_tiles(x):
    return jnp.transpose(jnp.stack([x[:, 128 * i : 128 * i + 128] for i in range(8)], axis=0), (1, 0, 2))


def tiles_to_rows(x):
    x = jnp.transpose(x, (1, 0, 2))
    return jnp.concatenate([x[i] for i in range(8)], axis=1)


S_IN, R_IN, L_IN = 0, 4, 8
S_OUT, R_OUT, L_OUT = 12, 16, 20
S_FIL, R_FIL, S_FG, R_FG, S_RS, R_RS, S_CX, R_CX, S_AG, R_AG = range(24, 34)
C_ARG, C_TAB, C_SMALL = 34, 38, 43
N_SEM = 49


def mixer_kernel(
    query, key, value, cot, skip, decay_h, w1_h, b1_h, w2_h, b2_h, w3_h, wide_h, thin_h, long_h, twid_h, feat_h,
    back, summed,
    q_v, k_v, v_v, g_v, decay, w1, b1, w2, b2, w3, wide, thin, long, twid, feat,
    send, recv, spec_s, spec_g, spec_f, corr, rows_f, out,
    w1a, w2a, h1a, c1, s2, c2, dec, env, fsend, frecv, gsend, grecv, draw, dact, m_feat, part, eighths, cx, agx, sem,
):
    me = lax.axis_index("ctx")
    tp = lax.axis_index("tp")

    def ring(step):
        return lax.rem(me + step, CTX)

    barrier = pltpu.get_barrier_semaphore()

    @pl.loop(1, CTX)
    def _(step):
        pl.semaphore_signal(barrier, inc=1, device_id={"ctx": ring(step)}, device_id_type=MESH)

    @pl.loop(1, TP)
    def _(step):
        pl.semaphore_signal(barrier, inc=1, device_id={"tp": lax.rem(tp + step, TP)}, device_id_type=MESH)

    def remote(src, dst, s, r, axis, j):
        return pltpu.make_async_remote_copy(
            src_ref=src, dst_ref=dst, send_sem=sem.at[s], recv_sem=sem.at[r], device_id={axis: j}, device_id_type=MESH
        )

    def local(src, dst, s):
        return pltpu.make_async_copy(src, dst, sem.at[s])

    def landed(ref, s):
        pltpu.make_async_copy(ref, ref, sem.at[s]).wait()

    loads = [local(a, b, C_ARG + i) for i, (a, b) in enumerate(((key, k_v), (value, v_v), (query, q_v), (cot, g_v)))]
    for c in loads:
        c.start()
    rest = [
        local(feat_h.at[:, pl.ds(pl.multiple_of(me * TOK, TOK), TOK)], feat.at[pl.ds(0, FROWS)], C_TAB),
        local(wide_h, wide, C_TAB + 1),
        local(thin_h, thin, C_TAB + 2),
        local(long_h, long, C_TAB + 3),
        local(twid_h, twid, C_TAB + 4),
    ]
    small = [
        local(a, b, C_SMALL + i)
        for i, (a, b) in enumerate(
            ((decay_h, decay), (w1_h, w1), (b1_h, b1), (w2_h, w2), (b2_h, b2), (w3_h, w3))
        )
    ]
    for c in rest[:1] + small + rest[1:]:
        c.start()

    def product(left, right, j, kind):
        rows = pl.ds(pl.multiple_of(j * OWN, OWN), OWN)
        x = left[rows, :].astype(F32) * right[rows, :].astype(F32)
        y = rows_to_tiles(x).reshape(16, 16, 128).astype(BF16)
        for p in range(16):
            send[2 * kind + p // 8, j, p % 8 // 2, :, 128 * (p % 2) : 128 * (p % 2) + 128] = y[p]

    def mine(rnd):
        return recv.at[rnd, :, pl.ds(pl.multiple_of(me * 16, 16), 16), :]

    def push(rnd, j):
        remote(send.at[rnd, j], mine(rnd), S_IN + rnd, R_IN + rnd, "ctx", j).start()

    def push_all(rnd):
        @pl.loop(1, CTX)
        def _(step):
            push(rnd, ring(step))

    loads[0].wait()
    loads[1].wait()
    product(k_v, v_v, me, 0)
    pl.semaphore_wait(barrier, CTX - 1 + TP - 1)

    @pl.loop(1, CTX)
    def _(step):
        product(k_v, v_v, ring(step), 0)
        push(0, ring(step))

    loads[2].wait()
    loads[3].wait()

    @pl.loop(0, CTX)
    def _(j):
        product(q_v, g_v, j, 1)

    push_all(2)
    own = [local(send.at[rnd, me], mine(rnd), L_IN + rnd) for rnd in range(4)]
    for c in own:
        c.start()

    rest[0].wait()
    for c in small:
        c.wait()
    feat[FROWS:, :] = jnp.zeros((64 - FROWS, TOK), F32)
    w1a[...] = jnp.zeros(w1a.shape, F32)
    w1a[0:EMB, :] = w1[...]
    w1a[EMB : EMB + 1, :] = b1[...]
    w2a[...] = jnp.zeros(w2a.shape, F32)
    w2a[0:ORDER, :] = w2[...]
    w2a[ORDER : ORDER + 1, :] = b2[...]
    h1a[ORDER:, :] = (lax.broadcasted_iota(jnp.int32, (8, TOK), 0) == 0).astype(F32)
    sine, cosine = sin_cos(dot_full(w1a[...], feat[0:FROWS, :], ((0,), (0,))))
    h1a[0:ORDER, :] = sine
    c1[...] = cosine
    sine, cosine = sin_cos(dot_full(w2a[...], h1a[...], ((0,), (0,))))
    s2[...] = sine
    c2[...] = cosine
    w3_own = pltpu.roll(w3[...], lax.rem(TP * GRL - tp * GRL, TP * GRL), 1)[:, 0:GRL]
    raw = dot_full(w3_own, s2[...], ((0,), (0,)))
    dec[...] = jnp.zeros(dec.shape, F32)
    dec[0:1, :] = decay[...]
    rate = dot_full(dec[...], h1a[ORDER:, :], ((0,), (0,)))
    position = (me * TOK + lax.broadcasted_iota(jnp.int32, (GRL, TOK), 1)).astype(F32)
    env[...] = jnp.exp(-position * rate) * jnp.sqrt(2.0 * rate + 1.0 / SEQ)
    fsend[...] = rows_to_tiles(raw * env[...]).reshape(CTX, 16, 128).astype(BF16)

    @pl.loop(1, CTX)
    def _(step):
        remote(fsend.at[ring(step)], frecv.at[me], S_FIL, R_FIL, "ctx", ring(step)).start()

    frecv[me] = fsend[me]
    push_all(1)

    for c in rest[1:]:
        c.wait()
    t_re = lambda: twid[0:256, :]
    t_im = lambda: twid[256:512, :]

    def forward_mid(first, pair):
        re = first[0:256, 128 * pair : 128 * pair + 128]
        im = first[256:512, 128 * pair : 128 * pair + 128]
        high, low = split(jnp.concatenate([re * t_re() - im * t_im(), re * t_im() + im * t_re()], axis=1))
        return dot(high, wide[1024:1280, :]) + dot(high, wide[1280:1536, :]) + dot(low, wide[1024:1280, :])

    def inverse_mid(spectra):
        res, ims = [], []
        for spectrum in spectra:
            high, low = split(spectrum)
            x = dot(high, wide[1536:1792, :]) + dot(high, wide[1792:2048, :]) + dot(low, wide[1536:1792, :])
            re, im = x[:, 0:128], x[:, 128:256]
            res.append(re * t_re() + im * t_im())
            ims.append(im * t_re() - re * t_im())
        return split(jnp.concatenate([jnp.concatenate(res, axis=1), jnp.concatenate(ims, axis=1)], axis=0))

    landed(frecv.at[pl.ds(0, CTX - 1)], R_FIL)
    taps = frecv[...].astype(F32).reshape(CTX, 2, 8, 128)
    taps = jnp.concatenate([taps[:, g].reshape(128, 128) for g in range(2)], axis=1).astype(BF16)
    first = dot(thin[0:512, :], taps) + dot(thin[512:1024, :], taps)
    for g in range(2):
        spec_f[g] = forward_mid(first, g)

    def arrived(rnd):
        own[rnd].wait()
        landed(recv.at[rnd, :, pl.ds(0, 240), :], R_IN + rnd)

    def forward(rnd, d, spec, g):
        x = recv[rnd, d]
        first = dot(wide[0:512, :], x) + dot(wide[512:1024, :], x)
        for pair in range(2):
            spec[g, d, pair] = forward_mid(first, pair)

    in_second = lax.broadcasted_iota(jnp.int32, (256, 128), 0) // 8 % 2 == 1

    def inverse(rnd, d, spec, g, sign):
        spectra = []
        for pair in range(2):
            re, im = spec[g, d, pair, :, 0:128], spec[g, d, pair, :, 128:256]
            f_re, f_im = spec_f[g, :, 0:128], sign * spec_f[g, :, 128:256]
            spectra.append(jnp.concatenate([re * f_re - im * f_im, re * f_im + im * f_re], axis=1))
        high, low = inverse_mid(spectra)
        y = dot(long[0:256, :], high) + dot(long[256:512, :], high) + dot(long[0:256, :], low)
        base = me * OWN + g * 16 + d * 4
        scale = jnp.concatenate(
            [jnp.where(in_second, skip[base + 2 * pair + 1], skip[base + 2 * pair]) for pair in range(2)], axis=1
        )
        rows_f[d] = y + scale * recv[rnd, d].astype(F32)

    def back_rows(rnd):
        return back.at[rnd // 2, pl.ds(pl.multiple_of(me * OWN + rnd % 2 * 16, 16), 16), :]

    def turn_all(rnd):
        @pl.loop(0, CTX)
        def _(j):
            block = pl.ds(pl.multiple_of(j * 16, 16), 16)
            tiles = [rows_f[d, block, 128 * p : 128 * p + 128] for d in range(4) for p in range(2)]
            out[rnd, j] = tiles_to_rows(jnp.stack(tiles, axis=0).reshape(16, 8, 128)).astype(BF16)

    kept = []

    def send_out(rnd):
        @pl.loop(1, CTX)
        def _(step):
            j = ring(step)
            remote(out.at[rnd, j], back_rows(rnd), S_OUT + rnd, R_OUT + rnd, "ctx", j).start()

        keep = local(out.at[rnd, me], back_rows(rnd), L_OUT + rnd)
        keep.start()
        kept.append(keep)

    def each_duo(*steps):
        @pl.loop(0, 4, unroll=4)
        def _(d):
            for step in steps:
                step(d)

    def forward_signal(g):
        return lambda d: forward(g, d, spec_s, g)

    def inverse_signal(g):
        return lambda d: inverse(g, d, spec_s, g, 1.0)

    def inverse_grad(g):
        return lambda d: inverse(2 + g, d, spec_g, g, -1.0)

    def forward_grad(g):
        corr[g] = jnp.zeros((256, 256), F32)

        def step(d):
            forward(2 + g, d, spec_g, g)
            for pair in range(2):
                s_re, s_im = spec_s[g, d, pair, :, 0:128], spec_s[g, d, pair, :, 128:256]
                g_re, g_im = spec_g[g, d, pair, :, 0:128], spec_g[g, d, pair, :, 128:256]
                corr[g, :, 0:128] += g_re * s_re + g_im * s_im
                corr[g, :, 128:256] += g_im * s_re - g_re * s_im

        return step

    arrived(0)
    push_all(3)
    each_duo(forward_signal(0), inverse_signal(0))
    turn_all(0)
    send_out(0)
    arrived(2)
    each_duo(forward_grad(0), inverse_grad(0))
    turn_all(2)
    arrived(1)
    send_out(2)
    each_duo(forward_signal(1))
    arrived(3)
    each_duo(forward_grad(1))

    high, low = inverse_mid([corr[0], corr[1]])
    taps = dot(long[512:640, :], high) + dot(long[640:768, :], high) + dot(long[512:640, :], low)
    taps = taps.reshape(CTX, 1, 8, 256)
    taps = jnp.concatenate([taps[..., 0:128], taps[..., 128:256]], axis=1)
    gsend[...] = taps.reshape(CTX, 16, 128).astype(BF16)

    @pl.loop(1, CTX)
    def _(step):
        remote(gsend.at[ring(step)], grecv.at[me], S_FG, R_FG, "ctx", ring(step)).start()

    grecv[me] = gsend[me]
    each_duo(inverse_signal(1))
    turn_all(1)

    landed(grecv.at[pl.ds(0, CTX - 1)], R_FG)
    got = grecv[...].astype(F32).reshape(GRL, 8, 128)
    draw[0:GRL, :] = tiles_to_rows(got) * (1.0 / math.sqrt(GSIZE * SEQ)) * env[...]
    draw[GRL:, :] = jnp.zeros((128 - GRL, TOK), F32)
    w3_own = pltpu.roll(w3[...], lax.rem(TP * GRL - tp * GRL, TP * GRL), 1)[:, 0:GRL]
    dact[0:ORDER, :] = dot_three(w3_own, draw[0:GRL, :], ((1,), (0,))) * c2[...]
    dact[ORDER:, :] = dot_three(w2[...], dact[0:ORDER, :], ((1,), (0,))) * c1[...]
    m_feat[...] = dot_three(feat[...], dact[...], ((1,), (1,)))
    m_feat[EMB + 1 : EMB + 2, :] = pltpu.roll(m_feat[...], ORDER, 1)[EMB : EMB + 1, :]
    g_hid = dot_three(h1a[0:ORDER, :], dact[...], ((1,), (1,)))
    lane = lax.broadcasted_iota(jnp.int32, (8, 128), 1)
    for k in range(TP):
        part[k] = jnp.where(lane < ORDER, g_hid[8 * k : 8 * k + 8, :], m_feat[5 * k : 5 * k + 8, :])

    @pl.loop(1, TP)
    def _(step):
        k = lax.rem(tp + step, TP)
        remote(part.at[k], eighths.at[tp], S_RS, R_RS, "tp", k).start()

    eighths[tp] = part[tp]
    g_out = dot_three(s2[...], draw[...], ((1,), (1,)))
    cx[me, 8:24, :] = sum(pltpu.roll(g_out[16 * i : 16 * i + 16, :], GRL * i, 1) for i in range(4))
    send_out(1)
    each_duo(inverse_grad(1))
    landed(eighths.at[pl.ds(0, TP - 1)], R_RS)
    cx[me, 0:8, :] = jnp.sum(eighths[...], axis=0)

    @pl.loop(1, CTX)
    def _(step):
        remote(cx.at[me], cx.at[me], S_CX, R_CX, "ctx", ring(step)).start()

    turn_all(3)
    send_out(3)
    landed(cx.at[pl.ds(0, CTX - 1)], R_CX)
    agx[tp] = jnp.sum(cx[...], axis=0)

    @pl.loop(1, TP)
    def _(step):
        remote(agx.at[tp], agx.at[tp], S_AG, R_AG, "tp", lax.rem(tp + step, TP)).start()

    landed(agx.at[pl.ds(0, TP - 1)], R_AG)
    summed[...] = agx[...]

    for c in kept:
        c.wait()
    for rnd in range(4):
        landed(back.at[rnd // 2, pl.ds(0, 240), :], R_OUT + rnd)
    for rnd in range(4):
        landed(send.at[rnd, pl.ds(0, CTX - 1)], S_IN + rnd)
        landed(out.at[rnd, pl.ds(0, CTX - 1)], S_OUT + rnd)
    landed(fsend.at[pl.ds(0, CTX - 1)], S_FIL)
    landed(gsend.at[pl.ds(0, CTX - 1)], S_FG)
    landed(part.at[pl.ds(0, TP - 1)], S_RS)
    landed(cx.at[pl.ds(0, CTX - 1)], S_CX)
    landed(agx.at[pl.ds(0, TP - 1)], S_AG)


def gate_kernel(
    query, key, value, cot, back, summed, mixed, g_query, g_key, g_value, o_w1, o_b1, o_w2, o_b2, o_w3,
    results, m_feat, sem_out,
):
    count = sem_out.shape[0]
    height = CHL // count
    stores = []
    for i in range(count):
        rows = slice(i * height, i * height + height)
        for kind, factors in enumerate(((query, cot), (value, key))):
            for k, factor in enumerate(factors):
                results[2 * kind + k, rows, :] = factor[rows, :] * back[kind, rows, :]
                target = (mixed, g_query, g_key, g_value)[2 * kind + k]
                c = pltpu.make_async_copy(
                    results.at[2 * kind + k, pl.ds(i * height, height), :],
                    target.at[pl.ds(i * height, height), :],
                    sem_out.at[i, 2 * kind + k],
                )
                c.start()
                stores.append(c)
    for k in range(TP):
        m_feat[5 * k : 5 * k + 5, :] = summed[k, 0:5, :]
        o_w2[8 * k : 8 * k + 8, :] = summed[k, 0:8, 0:ORDER]
    lane = lax.broadcasted_iota(jnp.int32, (16, 128), 1) // GRL
    for half in range(2):
        for i in range(4):
            block = jnp.zeros((16, 128), F32)
            for k in range(4):
                turned = pltpu.roll(summed[4 * half + k, 8:24, :], GRL * (k - i) % 128, 1)
                block = jnp.where(lane == k, turned, block)
            o_w3[16 * i : 16 * i + 16, 128 * half : 128 * half + 128] = block
    feat = pltpu.roll(m_feat[...], ORDER, 1)
    o_w1[...] = feat[0:EMB, 0:ORDER]
    o_b1[...] = feat[EMB : EMB + 1, 0:ORDER]
    o_b2[...] = feat[EMB + 1 : EMB + 2, 0:ORDER]
    for c in stores:
        c.wait()


def on_device(query, key, value, cot, skip, decay, w1, b1, w2, b2, w3):
    wide, thin, long, twid, feat = (jnp.asarray(t) for t in tables())
    f32 = lambda *shape: pltpu.VMEM(shape, F32)
    b16 = lambda *shape: pltpu.VMEM(shape, BF16)
    back, summed = pl.pallas_call(
        mixer_kernel,
        name="mixer",
        out_shape=(
            pltpu.VMEM((2, CHL, TOK), BF16),
            pltpu.VMEM((TP, 24, 128), F32),
        ),
        in_specs=[ANY] * 4 + [SMEM] + [ANY] * 11,
        out_specs=(VMEM, VMEM),
        scratch_shapes=[
            *[b16(CHL, TOK) for _ in range(4)],
            f32(1, GRL), f32(EMB, ORDER), f32(1, ORDER), f32(ORDER, ORDER), f32(1, ORDER), f32(ORDER, TP * GRL),
            b16(*wide.shape), b16(*thin.shape), b16(*long.shape), f32(*twid.shape), f32(64, TOK),
            b16(4, CTX, 4, 16, 256), b16(4, 4, 256, 256),
            f32(2, 4, 2, 256, 256), f32(2, 4, 2, 256, 256), f32(2, 256, 256), f32(2, 256, 256),
            f32(4, 256, 256), b16(4, CTX, 16, TOK),
            f32(FROWS, ORDER), f32(ORDER + 8, ORDER), f32(ORDER + 8, TOK), f32(ORDER, TOK), f32(ORDER, TOK),
            f32(ORDER, TOK), f32(8, GRL), f32(GRL, TOK),
            *[b16(CTX, 16, 128) for _ in range(4)],
            f32(128, TOK), f32(128, TOK), f32(ORDER, 128),
            f32(TP, 8, 128), f32(TP, 8, 128), f32(CTX, 24, 128), f32(TP, 24, 128),
            pltpu.SemaphoreType.DMA((N_SEM,)),
        ],
        compiler_params=pltpu.CompilerParams(
            collective_id=0, has_side_effects=True, vmem_limit_bytes=56 * 1024 * 1024
        ),
        cost_estimate=pl.CostEstimate(flops=12_000_000_000, bytes_accessed=10_000_000, transcendentals=200_000),
    )(query, key, value, cot, skip, decay[None], w1, b1[None], w2, b2[None], w3, wide, thin, long, twid, feat)
    chunks = 4
    mixed, g_query, g_key, g_value, o_w1, o_b1, o_w2, o_b2, o_w3 = pl.pallas_call(
        gate_kernel,
        name="gates",
        out_shape=tuple(jax.ShapeDtypeStruct((CHL, TOK), BF16) for _ in range(4))
        + tuple(
            jax.ShapeDtypeStruct(s, F32)
            for s in ((EMB, ORDER), (1, ORDER), (ORDER, ORDER), (1, ORDER), (ORDER, TP * GRL))
        ),
        in_specs=[VMEM] * 6,
        out_specs=(ANY,) * 4 + (VMEM,) * 5,
        scratch_shapes=[
            b16(4, CHL, TOK), f32(FROWS, 128), pltpu.SemaphoreType.DMA((chunks, 4)),
        ],
        compiler_params=pltpu.CompilerParams(vmem_limit_bytes=32 * 1024 * 1024),
        cost_estimate=pl.CostEstimate(flops=4_000_000, bytes_accessed=11_000_000, transcendentals=0),
    )(query, key, value, cot, back, summed)
    return mixed, g_query, g_key, g_value, o_w1, o_b1[0], o_w2, o_b2[0], o_w3


def solution(mesh):
    sharded = P("tp", "ctx")
    return jax.shard_map(
        on_device,
        mesh=mesh,
        in_specs=(sharded,) * 4 + (P("tp"), P("tp")) + (P(),) * 5,
        out_specs=(sharded,) * 4 + (P(),) * 5,
        check_vma=False,
    )
```
